512 devices in a mesh: slab: 32 (over x_hi, z, core), grp: 16 (over y, x_lo).
Axes of the slice: x: 4 (x_hi: 2, x_lo: 2; x = x_hi * 2 + x_lo), y: 8, z: 8, core: 2. Of those that a mesh axis runs over, the one named last changes fastest.
Arguments:
- comp: float32 [4096, 128, 128], P(('slab', 'grp')), may hold values from -1 to 1
- guess: float32 [1024, 32, 32], P('slab', 'grp'), may hold values from -3 to 3
Outputs:
- comp_next: float32 [4096, 128, 128], P(('slab', 'grp'))
- potential: float32 [1024, 32, 32], P('slab', 'grp')
The draws below stay inside these ranges and needn't reach their ends.
All inputs are finite; a program needn't handle non-finite values.
Results may differ from the reference program's by a relative error of at most 0.00002.
Values sent between devices are 32-bit elements; how exact they have to be, the bound alone decides.
A program may use at most 64 MiB of HBM per device.

```python
import jax
import jax.numpy as jnp

NY = 128
NZ = 128
NPRE = 1
NCOARSE = 3
NPOST = 2
NX = 4096
CNX = 1024
CNY = 32
CNZ = 32


def level_of(key, shape, split, low, largest):
    level = 1.0
    for dim, shards_of in split:
        steps = jax.random.uniform(jax.random.fold_in(jax.random.fold_in(key, 6), dim), (shards_of,), jnp.float32, low / len(split), largest / len(split))
        level = level * jnp.repeat(jnp.exp(steps), shape[dim] // shards_of).reshape((-1,) + (1,) * (len(shape) - 1 - dim))
    return level


def gaussian(rng, dims, deviation, limit, shards=(), kind=jnp.bfloat16):
    values = deviation * jax.random.normal(rng, dims, jnp.float32)
    if shards:
        values = values * level_of(rng, dims, shards, -0.22, 0.18)
    return jnp.clip(values, -limit, limit).astype(kind)


def setup_inputs(seed: int = 0) -> dict:
    key_list = jax.random.split(jax.random.key(seed), 3)
    comp = jnp.clip(jax.random.uniform(key_list[0], (NX, NY, NZ), jnp.float32, -1.0, 1.0) * level_of(key_list[0], (NX, NY, NZ), ((0, 512),), -0.4, 0.0), -1.0, 1.0)
    guess = gaussian(key_list[1], (CNX, CNY, CNZ), 0.5, 3.0, ((0, 32), (1, 16)), jnp.float32)
    return {"comp": comp, "guess": guess}


gradient_energy = 0.5
screening = 0.5
damping = 0.8
long_range = 4.0
time_step = 0.02


def laplace_padded(padded):
    inner = padded[1:-1, 1:-1, 1:-1]
    beside_all = padded[2:, 1:-1, 1:-1] + padded[:-2, 1:-1, 1:-1]
    beside_all = beside_all + padded[1:-1, 2:, 1:-1] + padded[1:-1, :-2, 1:-1]
    beside_all = beside_all + padded[1:-1, 1:-1, 2:] + padded[1:-1, 1:-1, :-2]
    return beside_all - 6.0 * inner


def laplace(field):
    return laplace_padded(jnp.pad(field, 1))


def block_mean(field, factor):
    first, second, third = field.shape
    return field.reshape(first // factor, factor, second // factor, factor, third // factor, factor).mean(axis=(1, 3, 5))


def expand(field, factor):
    first, second, third = field.shape
    wide = jnp.broadcast_to(field[:, None, :, None, :, None], (first, factor, second, factor, third, factor))
    return wide.reshape(first * factor, second * factor, third * factor)


def smooth(potential, source):
    operated = screening * potential - laplace(potential)
    return potential + damping * (source - operated) / (screening + 6.0)


def reference(comp, guess):
    chem = comp * comp * comp - comp - gradient_energy * laplace(comp)
    source = block_mean(comp, 4)
    potential = guess
    for sweep in range(NPRE):
        potential = smooth(potential, source)
    residual = source - (screening * potential - laplace(potential))
    coarsest = block_mean(residual, 2)
    correction = damping * coarsest / (screening + 1.5)
    for sweep in range(NCOARSE - 1):
        operated = screening * correction - 0.25 * laplace(correction)
        correction = correction + damping * (coarsest - operated) / (screening + 1.5)
    potential = potential + expand(correction, 2)
    for sweep in range(NPOST):
        potential = smooth(potential, source)
    field = chem + long_range * expand(potential, 4)
    comp_next = comp + time_step * laplace(field)
    return comp_next, potential
```

```python
import jax
import jax.numpy as jnp
from jax import lax
from jax.experimental import pallas as pl
from jax.experimental.pallas import tpu as pltpu
from jax.sharding import PartitionSpec as P

MESH = pl.DeviceIdType.MESH
REACH = 5
WINDOW = 2 * REACH + 1
F32 = jnp.float32
BF16 = jnp.bfloat16


def iota(shape, dim):
    return lax.broadcasted_iota(jnp.int32, shape, dim)


def lanes(x, shift):
    return pltpu.roll(x, (-shift) % 128, 1)


def rows(x, shift):
    return pltpu.roll(x, (-shift) % x.shape[0], 0)


def split3(x):
    high = x.astype(BF16)
    rest = x - high.astype(F32)
    mid = rest.astype(BF16)
    low = (rest - mid.astype(F32)).astype(BF16)
    return high, mid, low


def neighbours(v, first, last):
    own = v[16:-16]
    lane, row = iota(own.shape, 1), iota(own.shape, 0) % 16
    a, b = lanes(own, 32), lanes(own, -32)
    up = jnp.where(row < 15, rows(b, 1), 0.0)
    down = jnp.where(row > 0, rows(a, -1), 0.0)
    total = jnp.where(lane % 64 < 32, a + down, b + up)
    total += jnp.where(lane % 32 < 31, lanes(own, 1), 0.0)
    total += jnp.where(lane % 32 > 0, lanes(own, -1), 0.0)
    h = pltpu.roll(v, 64, 1)
    return total + h[16:-16] + jnp.where(lane < 64, h[:-32], h[32:])


def coarse_cycle(source, guess, first_pair, pairs):
    def inside(v, first):
        pair = first_pair + first + iota(v.shape, 0) // 16
        return jnp.where((pair >= 0) & (pair < pairs), v, 0.0)

    def sweep(v, s):
        return 0.2 * v[16:-16] + (0.8 / 6.5) * (s + neighbours(v, 0, 0))

    guess = inside(guess, 0)
    source = inside(source, 0)
    edge = jnp.zeros((16, 128), F32)
    pre = inside(sweep(jnp.concatenate([edge, guess, edge], 0), source), 0)
    resid = inside(source[16:-16] + neighbours(pre, 0, 0) - 6.5 * pre[16:-16], 1)
    lane = iota(resid.shape, 1)
    t = resid + pltpu.roll(resid, 64, 1)
    t = t + jnp.where(lane % 64 < 32, lanes(t, 32), lanes(t, -32))
    t = t + jnp.where(lane % 2 < 1, lanes(t, 1), lanes(t, -1))
    start = t * 0.05
    c, first = start, 1
    for _ in range(2):
        own = c[16:-16]
        lane, row = iota(own.shape, 1) % 32, iota(own.shape, 0) % 16
        total = c[:-32] + c[32:]
        total += jnp.where(row < 15, rows(own, 1), 0.0) + jnp.where(row > 0, rows(own, -1), 0.0)
        total += jnp.where(lane < 30, lanes(own, 2), 0.0) + jnp.where(lane > 1, lanes(own, -2), 0.0)
        first = first + 1
        c = inside(0.2 * own + start[16 * (first - 1) : -16 * (first - 1)] + 0.1 * total, first)
    mid = inside(pre[16 * first : -16 * first] + c, first)
    mid = inside(sweep(mid, source[16 * (first + 1) : -16 * (first + 1)]), first + 1)
    edge = jnp.zeros((16, 128), F32)
    mid = jnp.concatenate([edge, mid, edge], 0)
    return inside(sweep(mid, source[16 * (first + 1) : -16 * (first + 1)]), first + 1)


def plane_neighbours(v):
    row, lane = iota(v.shape, 0), iota(v.shape, 1)
    total = jnp.where(row < 127, rows(v, 1), 0.0) + jnp.where(row > 0, rows(v, -1), 0.0)
    total += jnp.where(lane < 127, lanes(v, 1), 0.0) + jnp.where(lane > 0, lanes(v, -1), 0.0)
    return total


def spread(fine, coarse):
    block, place = fine // 4, fine % 4
    same = jnp.where(block == coarse, 1.0, 0.0)
    first, last = jnp.where(place == 0, 1.0, 0.0), jnp.where(place == 3, 1.0, 0.0)
    second = -same * (first + last)
    second += first * jnp.where(block - 1 == coarse, 1.0, 0.0)
    second += last * jnp.where(block + 1 == coarse, 1.0, 0.0)
    return same, second


def step(
    slabs, comp, guess, out, pot, cells, given, lines, window, chem, sums, gather, z_mat, y_mat,
    potline, cell_sem, given_sem, line_send, line_recv, near_send, near_recv, halo_send,
    halo_recv, pot_send, pot_recv,
):
    s, g = lax.axis_index("slab"), lax.axis_index("grp")
    me = s * 16 + g
    pairs = slabs * 16

    def device(d):
        return (d // 16, d % 16)

    halves = [
        pltpu.make_async_copy(comp.at[4 * h : 4 * h + 4], cells.at[2 + 4 * h : 6 + 4 * h], cell_sem.at[h])
        for h in range(2)
    ]
    load_guess = pltpu.make_async_copy(guess, given, given_sem)
    load_guess.start()
    for half in halves:
        half.start()

    barrier = pltpu.get_barrier_semaphore()
    crossing = jnp.int32(15)
    for k in range(1, REACH + 1):
        for d, across in ((me + k, g + k > 15), (me - k, g - k < 0)):
            other = across & (d >= 0) & (d < pairs)
            crossing += other.astype(jnp.int32)

            @pl.when(other)
            def _():
                pl.semaphore_signal(barrier, 1, device_id=device(d), device_id_type=MESH)

    for k in range(1, 16):
        pl.semaphore_signal(barrier, 1, device_id=(s, (g + k) % 16), device_id_type=MESH)

    load_guess.wait()
    packed = given.reshape(64, 32)
    lines[...] = jnp.concatenate([packed[pl.ds(k, 16, stride=4), :] for k in range(4)], axis=1)

    pl.semaphore_wait(barrier, crossing)
    for k in range(1, 16):
        to = (g + k) % 16
        pltpu.make_async_remote_copy(
            lines.at[pl.ds(to, 1)], window.at[REACH, 1, pl.ds(g, 1)], line_send, line_recv,
            device_id=(s, to), device_id_type=MESH,
        ).start()
    window[REACH, 1, pl.ds(g, 1), :] = lines[pl.ds(g, 1), :]

    at, lane = iota((512, 128), 0), iota((512, 128), 1)
    hit = (at // 128 == lane // 32) & (at % 128 // 4 == lane % 32)
    gather[...] = jnp.where(hit, 1.0 / 64, 0.0).astype(BF16)
    for h in range(2):
        halves[h].wait()
        own = 2 + 4 * h
        sums[h] = (cells[own] + cells[own + 1]) + (cells[own + 2] + cells[own + 3])
    parts = []
    for h in range(2):
        for half in range(2):
            parts.append(sum(sums[h, pl.ds(4 * half + j, 16, stride=8), :] for j in range(4)))
    wide = jnp.concatenate(split3(jnp.concatenate(parts, axis=1)), axis=0)
    means = jnp.dot(wide, gather[...], preferred_element_type=F32)
    window[REACH, 0] = means[:16] + means[16:32] + means[32:]

    fifteen = pltpu.make_async_remote_copy(
        lines.at[pl.ds(0, 15)], window.at[REACH, 1, pl.ds(0, 15)], line_send, line_recv,
        device_id=(s, (g + 1) % 16), device_id_type=MESH,
    )
    fifteen.wait_recv()
    near = []
    for k in range(1, REACH + 1):
        for i, o in ((2 * k - 2, k), (2 * k - 1, -k)):
            copy = pltpu.make_async_remote_copy(
                window.at[REACH], window.at[REACH - o], near_send.at[i], near_recv.at[i],
                device_id=device(me + o), device_id_type=MESH,
            )
            goes = (me + o >= 0) & (me + o < pairs)
            comes = (me - o >= 0) & (me - o < pairs)
            pl.when(goes)(copy.start)
            near.append((copy, goes, comes))

    halo = []
    for i, (o, src, dst) in enumerate(((1, comp.at[6:8], cells.at[0:2]), (-1, comp.at[0:2], cells.at[10:12]))):
        copy = pltpu.make_async_remote_copy(
            src, dst, halo_send.at[i], halo_recv.at[i], device_id=device(me + o), device_id_type=MESH
        )
        goes = (me + o >= 0) & (me + o < pairs)
        comes = (me - o >= 0) & (me - o < pairs)
        pl.when(goes)(copy.start)
        halo.append((copy, goes, comes))

    at, lane = iota((128, 512), 0), iota((128, 512), 1)
    hit = (lane // 128 == at // 32) & (lane % 128 // 4 == at % 32)
    z_mat[0] = jnp.where(hit, 1.0, 0.0).astype(BF16)
    z_mat[1] = jnp.where(hit & (lane % 4 == 0), 1.0, 0.0).astype(BF16)
    z_mat[2] = jnp.where(hit & (lane % 4 == 3), 1.0, 0.0).astype(BF16)
    at, lane = iota((128, 192), 0), iota((128, 192), 1)
    coarse = 2 * (lane % 16) + (lane // 16) % 2
    same, second = spread(at, coarse)
    y_mat[...] = jnp.where(lane < 96, second, same).astype(BF16)

    def chemical(p):
        u = cells[p + 2]
        around = cells[p + 1] + cells[p + 3] + plane_neighbours(u)
        chem[p + 1] = u * u * u + 2.0 * u - 0.5 * around

    def partial(f):
        mu = chem[f + 1]
        around = chem[f] + chem[f + 2] + plane_neighbours(mu)
        out[f] = cells[f + 2] + 0.02 * (around - 6.0 * mu)

    lax.fori_loop(1, 7, lambda p, _: (chemical(p), 0)[1], 0)
    lax.fori_loop(2, 6, lambda f, _: (partial(f), 0)[1], 0)

    for copy, goes, comes in near:
        pl.when(comes)(copy.wait_recv)
    potential = coarse_cycle(
        window[:, 0].reshape(WINDOW * 16, 128), window[:, 1].reshape(WINDOW * 16, 128), me - REACH, pairs
    )
    centre = potential[16:32]
    lines_p = potline
    lines_p[...] = centre
    for k in range(1, 16):
        to = (g + k) % 16
        pltpu.make_async_remote_copy(
            lines_p.at[pl.ds(to, 1)], pot.at[pl.ds(g, 1)], pot_send, pot_recv,
            device_id=(s, to), device_id_type=MESH,
        ).start()
    pot[pl.ds(g, 1), :] = lines_p[pl.ds(g, 1), :]

    lane = iota((16, 128), 1)
    swapped = pltpu.roll(potential, 64, 1)
    before = jnp.where(lane < 64, swapped[:16], swapped[16:32]) - centre
    after = jnp.where(lane < 64, swapped[16:32], swapped[32:]) - centre
    left = jnp.where(lane % 32 > 0, lanes(centre, -1), 0.0) - centre
    right = jnp.where(lane % 32 < 31, lanes(centre, 1), 0.0) - centre
    t0 = jnp.dot(
        jnp.concatenate(split3(centre) + split3(before) + split3(after), 0), z_mat[0],
        preferred_element_type=F32,
    ).astype(BF16)
    t1 = jnp.dot(
        jnp.concatenate([jnp.concatenate(split3(left), 0), jnp.concatenate(split3(right), 0)], 1),
        z_mat[1:].reshape(256, 512), preferred_element_type=F32,
    ).astype(BF16)

    def stacked(t, at, column):
        return [
            t[at + 16 * i : at + 16 * i + 16, column + 128 * py : column + 128 * py + 128]
            for i in range(3)
            for py in range(2)
        ]

    for copy, goes, comes in halo:
        pl.when(comes)(copy.wait_recv)
    zero = jnp.zeros((2, 128, 128), F32)

    @pl.when(me == 0)
    def _():
        cells[0:2] = zero

    @pl.when(me == pairs - 1)
    def _():
        cells[10:12] = zero

    for p in (-1, 0, 7, 8):
        chemical(p)

    @pl.when(me == 0)
    def _():
        chem[0] = zero[0]

    @pl.when(me == pairs - 1)
    def _():
        chem[9] = zero[0]

    for f in (0, 1, 6, 7):
        partial(f)

    for px in range(2):
        rhs = jnp.concatenate(stacked(t0, 0, 256 * px) + stacked(t1, 0, 256 * px), 0)
        base = 0.08 * jnp.dot(y_mat[...], rhs, preferred_element_type=F32)
        low = 0.08 * jnp.dot(
            y_mat[:, 96:], jnp.concatenate(stacked(t0, 48, 256 * px), 0), preferred_element_type=F32
        )
        high = 0.08 * jnp.dot(
            y_mat[:, 96:], jnp.concatenate(stacked(t0, 96, 256 * px), 0), preferred_element_type=F32
        )
        out[4 * px] += base + low
        out[4 * px + 1] += base
        out[4 * px + 2] += base
        out[4 * px + 3] += base + high

    done = pltpu.make_async_remote_copy(
        lines_p.at[pl.ds(0, 15)], pot.at[pl.ds(0, 15)], pot_send, pot_recv,
        device_id=(s, (g + 1) % 16), device_id_type=MESH,
    )
    done.wait_recv()
    fifteen.wait_send()
    done.wait_send()
    for copy, goes, comes in near + halo:
        pl.when(goes)(copy.wait_send)


def unpack(fine, lines, out, pot, sem):
    copy = pltpu.make_async_copy(fine, out, sem)
    copy.start()
    packed = pot.reshape(64, 32)
    for k in range(4):
        packed[pl.ds(k, 16, stride=4), :] = lines[:, 32 * k : 32 * k + 32]
    copy.wait()


def per_device(comp, guess):
    slabs = lax.axis_size("slab")
    dma = pltpu.SemaphoreType.DMA

    def body(*refs):
        step(slabs, *refs)

    vmem = pl.BlockSpec(memory_space=pltpu.VMEM)
    anywhere = pl.BlockSpec(memory_space=pl.ANY)
    fine, lines = pl.pallas_call(
        body,
        out_shape=(jax.ShapeDtypeStruct((8, 128, 128), F32), jax.ShapeDtypeStruct((16, 128), F32)),
        in_specs=[pl.BlockSpec(memory_space=pltpu.HBM)] * 2,
        out_specs=(vmem, vmem),
        scratch_shapes=[
            pltpu.VMEM((12, 128, 128), F32),
            pltpu.VMEM((32, 2, 32), F32),
            pltpu.VMEM((16, 128), F32),
            pltpu.VMEM((WINDOW, 2, 16, 128), F32),
            pltpu.VMEM((10, 128, 128), F32),
            pltpu.VMEM((2, 128, 128), F32),
            pltpu.VMEM((512, 128), BF16),
            pltpu.VMEM((3, 128, 512), BF16),
            pltpu.VMEM((128, 192), BF16),
            pltpu.VMEM((16, 128), F32),
            dma((2,)),
            dma,
            dma,
            dma,
            dma((2 * REACH,)),
            dma((2 * REACH,)),
            dma((2,)),
            dma((2,)),
            dma,
            dma,
        ],
        compiler_params=pltpu.CompilerParams(
            collective_id=0, has_side_effects=True, vmem_limit_bytes=32 * 1024 * 1024
        ),
        name="step",
    )(comp, guess)
    return pl.pallas_call(
        unpack,
        out_shape=(jax.ShapeDtypeStruct(comp.shape, F32), jax.ShapeDtypeStruct(guess.shape, F32)),
        in_specs=[vmem, vmem],
        out_specs=(pl.BlockSpec(memory_space=pltpu.HBM), vmem),
        scratch_shapes=[dma],
        name="unpack",
    )(fine, lines)


def solution(mesh):
    placed = (P(("slab", "grp"), None, None), P("slab", "grp", None))
    return jax.shard_map(
        per_device, mesh=mesh, in_specs=placed, out_specs=placed, check_vma=False
    )
```

```python
import jax
import jax.numpy as jnp
from jax import lax
from jax.experimental import pallas as pl
from jax.experimental.pallas import tpu as pltpu
from jax.sharding import PartitionSpec as P

MESH = pl.DeviceIdType.MESH
REACH = 5
WINDOW = 2 * REACH + 1
FAR_FIRST = (8, 7, 9, 6, 10, 5, 11, 4, 12, 3, 13, 2, 14, 1, 15)
F32 = jnp.float32
BF16 = jnp.bfloat16


def iota(shape, dim):
    return lax.broadcasted_iota(jnp.int32, shape, dim)


def lanes(x, shift):
    return pltpu.roll(x, (-shift) % 128, 1)


def rows(x, shift):
    return pltpu.roll(x, (-shift) % x.shape[0], 0)


def split3(x):
    high = x.astype(BF16)
    rest = x - high.astype(F32)
    mid = rest.astype(BF16)
    low = (rest - mid.astype(F32)).astype(BF16)
    return high, mid, low


def neighbours(v, first, last):
    own = v[16:-16]
    lane, row = iota(own.shape, 1), iota(own.shape, 0) % 16
    a, b = lanes(own, 32), lanes(own, -32)
    up = jnp.where(row < 15, rows(b, 1), 0.0)
    down = jnp.where(row > 0, rows(a, -1), 0.0)
    total = jnp.where(lane % 64 < 32, a + down, b + up)
    total += jnp.where(lane % 32 < 31, lanes(own, 1), 0.0)
    total += jnp.where(lane % 32 > 0, lanes(own, -1), 0.0)
    h = pltpu.roll(v, 64, 1)
    return total + h[16:-16] + jnp.where(lane < 64, h[:-32], h[32:])


def coarse_cycle(source, guess, first_pair, pairs):
    def inside(v, first):
        pair = first_pair + first + iota(v.shape, 0) // 16
        return jnp.where((pair >= 0) & (pair < pairs), v, 0.0)

    def sweep(v, s):
        return 0.2 * v[16:-16] + (0.8 / 6.5) * (s + neighbours(v, 0, 0))

    guess = inside(guess, 0)
    source = inside(source, 0)
    edge = jnp.zeros((16, 128), F32)
    pre = inside(sweep(jnp.concatenate([edge, guess, edge], 0), source), 0)
    resid = inside(source[16:-16] + neighbours(pre, 0, 0) - 6.5 * pre[16:-16], 1)
    lane = iota(resid.shape, 1)
    t = resid + pltpu.roll(resid, 64, 1)
    t = t + jnp.where(lane % 64 < 32, lanes(t, 32), lanes(t, -32))
    t = t + jnp.where(lane % 2 < 1, lanes(t, 1), lanes(t, -1))
    start = t * 0.05
    c, first = start, 1
    for _ in range(2):
        own = c[16:-16]
        lane, row = iota(own.shape, 1) % 32, iota(own.shape, 0) % 16
        total = c[:-32] + c[32:]
        total += jnp.where(row < 15, rows(own, 1), 0.0) + jnp.where(row > 0, rows(own, -1), 0.0)
        total += jnp.where(lane < 30, lanes(own, 2), 0.0) + jnp.where(lane > 1, lanes(own, -2), 0.0)
        first = first + 1
        c = inside(0.2 * own + start[16 * (first - 1) : -16 * (first - 1)] + 0.1 * total, first)
    mid = inside(pre[16 * first : -16 * first] + c, first)
    mid = inside(sweep(mid, source[16 * (first + 1) : -16 * (first + 1)]), first + 1)
    edge = jnp.zeros((16, 128), F32)
    mid = jnp.concatenate([edge, mid, edge], 0)
    return inside(sweep(mid, source[16 * (first + 1) : -16 * (first + 1)]), first + 1)


def plane_neighbours(v):
    row, lane = iota(v.shape, 0), iota(v.shape, 1)
    total = jnp.where(row < 127, rows(v, 1), 0.0) + jnp.where(row > 0, rows(v, -1), 0.0)
    total += jnp.where(lane < 127, lanes(v, 1), 0.0) + jnp.where(lane > 0, lanes(v, -1), 0.0)
    return total


def spread(fine, coarse):
    block, place = fine // 4, fine % 4
    same = jnp.where(block == coarse, 1.0, 0.0)
    first, last = jnp.where(place == 0, 1.0, 0.0), jnp.where(place == 3, 1.0, 0.0)
    second = -same * (first + last)
    second += first * jnp.where(block - 1 == coarse, 1.0, 0.0)
    second += last * jnp.where(block + 1 == coarse, 1.0, 0.0)
    return same, second


def step(
    slabs, comp, guess, out, pot, cells, given, lines, sources, guesses, beyond, chem, sums, gather, z_mat,
    y_mat, centre, cell_sem, given_sem, line_send, line_recv, cross_send, cross_recv, near_send, near_recv,
    halo_send, halo_recv, pot_send, pot_recv,
):
    s, g = lax.axis_index("slab"), lax.axis_index("grp")
    me = s * 16 + g
    pairs = slabs * 16
    below, above = s > 0, s < slabs - 1
    from_below, from_above = below & (g < REACH), above & (g >= 16 - REACH)

    def device(d):
        return (d // 16, d % 16)

    halves = [
        pltpu.make_async_copy(comp.at[4 * h : 4 * h + 4], cells.at[2 + 4 * h : 6 + 4 * h], cell_sem.at[h])
        for h in range(2)
    ]
    load_guess = pltpu.make_async_copy(guess, given, given_sem)
    load_guess.start()
    for half in halves:
        half.start()

    barrier = pltpu.get_barrier_semaphore()
    for there, other in ((from_below, s - 1), (from_above, s + 1)):

        @pl.when(there)
        def _():
            for k in range(16):
                pl.semaphore_signal(barrier, 1, device_id=(other, (g + k) % 16), device_id_type=MESH)

    for k in FAR_FIRST:
        pl.semaphore_signal(barrier, 1, device_id=(s, (g + k) % 16), device_id_type=MESH)

    load_guess.wait()
    packed = given.reshape(64, 32)
    lines[0:REACH] = jnp.zeros((REACH, 128), F32)
    lines[REACH + 16 :] = jnp.zeros((REACH, 128), F32)
    lines[REACH : REACH + 16] = jnp.concatenate(
        [packed[pl.ds(k, 16, stride=4), :] for k in range(4)], axis=1
    )

    at, lane = iota((512, 128), 0), iota((512, 128), 1)
    hit = (at // 128 == lane // 32) & (at % 128 // 4 == lane % 32)
    gather[...] = jnp.where(hit, 1.0 / 64, 0.0).astype(BF16)
    for h in range(2):
        halves[h].wait()
        own = 2 + 4 * h
        sums[h] = (cells[own] + cells[own + 1]) + (cells[own + 2] + cells[own + 3])
    parts = []
    for h in range(2):
        for half in range(2):
            parts.append(sum(sums[h, pl.ds(4 * half + j, 16, stride=8), :] for j in range(4)))
    wide = jnp.concatenate(split3(jnp.concatenate(parts, axis=1)), axis=0)
    means = jnp.dot(wide, gather[...], preferred_element_type=F32)
    sources[REACH] = means[:16] + means[16:32] + means[32:]

    pl.semaphore_wait(
        barrier, 15 + REACH * (below.astype(jnp.int32) + above.astype(jnp.int32))
    )

    @pl.when(above)
    def _():
        for to in range(REACH):
            pltpu.make_async_remote_copy(
                lines.at[16 + to : 21], beyond.at[0 : REACH - to, g], cross_send.at[0], cross_recv,
                device_id=(s + 1, to), device_id_type=MESH,
            ).start()

    @pl.when(below)
    def _():
        for to in range(16 - REACH, 16):
            pltpu.make_async_remote_copy(
                lines.at[REACH : to - 5], beyond.at[21 - to : WINDOW, g], cross_send.at[1], cross_recv,
                device_id=(s - 1, to), device_id_type=MESH,
            ).start()

    for k in FAR_FIRST:
        to = (g + k) % 16
        pltpu.make_async_remote_copy(
            lines.at[pl.ds(to, WINDOW)], guesses.at[:, g], line_send, line_recv,
            device_id=(s, to), device_id_type=MESH,
        ).start()
    guesses[:, pl.ds(g, 1), :] = lines[pl.ds(g, WINDOW), :].reshape(WINDOW, 1, 128)

    near = []
    for k in range(REACH, 0, -1):
        for i, o in ((2 * k - 2, k), (2 * k - 1, -k)):
            copy = pltpu.make_async_remote_copy(
                sources.at[REACH], sources.at[REACH - o], near_send.at[i], near_recv.at[i],
                device_id=device(me + o), device_id_type=MESH,
            )
            goes = (me + o >= 0) & (me + o < pairs)
            comes = (me - o >= 0) & (me - o < pairs)
            pl.when(goes)(copy.start)
            near.append((copy, goes, comes))

    halo = []
    for i, (o, src, dst) in enumerate(((1, comp.at[6:8], cells.at[0:2]), (-1, comp.at[0:2], cells.at[10:12]))):
        copy = pltpu.make_async_remote_copy(
            src, dst, halo_send.at[i], halo_recv.at[i], device_id=device(me + o), device_id_type=MESH
        )
        goes = (me + o >= 0) & (me + o < pairs)
        comes = (me - o >= 0) & (me - o < pairs)
        pl.when(goes)(copy.start)
        halo.append((copy, goes, comes))

    at, lane = iota((128, 512), 0), iota((128, 512), 1)
    hit = (lane // 128 == at // 32) & (lane % 128 // 4 == at % 32)
    z_mat[0] = jnp.where(hit, 1.0, 0.0).astype(BF16)
    z_mat[1] = jnp.where(hit & (lane % 4 == 0), 1.0, 0.0).astype(BF16)
    z_mat[2] = jnp.where(hit & (lane % 4 == 3), 1.0, 0.0).astype(BF16)
    at, lane = iota((128, 192), 0), iota((128, 192), 1)
    coarse = 2 * (lane % 16) + (lane // 16) % 2
    same, second = spread(at, coarse)
    y_mat[...] = jnp.where(lane < 96, second, same).astype(BF16)

    def chemical(p):
        u = cells[p + 2]
        around = cells[p + 1] + cells[p + 3] + plane_neighbours(u)
        chem[p + 1] = u * u * u + 2.0 * u - 0.5 * around

    def partial(f):
        mu = chem[f + 1]
        around = chem[f] + chem[f + 2] + plane_neighbours(mu)
        out[f] = cells[f + 2] + 0.02 * (around - 6.0 * mu)

    lax.fori_loop(1, 7, lambda p, _: (chemical(p), 0)[1], 0)
    lax.fori_loop(2, 6, lambda f, _: (partial(f), 0)[1], 0)

    lines_in = pltpu.make_async_remote_copy(
        guesses.at[:, 0:15], guesses.at[:, 0:15], line_send, line_recv,
        device_id=(s, (g + 1) % 16), device_id_type=MESH,
    )
    lines_in.wait_recv()
    for there, spots in (
        (from_below, [(j, slice(0, REACH - j)) for j in range(REACH)]),
        (from_above, [(j, slice(21 - j, WINDOW)) for j in range(16 - REACH, 16)]),
    ):
        for j, spot in spots:

            @pl.when(there & (g == j))
            def _():
                pltpu.make_async_remote_copy(
                    beyond.at[spot], beyond.at[spot], cross_send.at[0], cross_recv,
                    device_id=(s, (g + 1) % 16), device_id_type=MESH,
                ).wait_recv()

    for copy, goes, comes in near:
        pl.when(comes)(copy.wait_recv)
    place = g - REACH + iota((WINDOW * 16, 128), 0) // 16
    start = jnp.where(
        (place >= 0) & (place < 16), guesses[...].reshape(WINDOW * 16, 128), beyond[...].reshape(WINDOW * 16, 128)
    )
    potential = coarse_cycle(sources[...].reshape(WINDOW * 16, 128), start, me - REACH, pairs)
    own = potential[16:32]
    centre[...] = own
    for k in FAR_FIRST:
        to = (g + k) % 16
        pltpu.make_async_remote_copy(
            centre.at[pl.ds(to, 1)], pot.at[pl.ds(g, 1)], pot_send, pot_recv,
            device_id=(s, to), device_id_type=MESH,
        ).start()
    pot[pl.ds(g, 1), :] = centre[pl.ds(g, 1), :]

    lane = iota((16, 128), 1)
    swapped = pltpu.roll(potential, 64, 1)
    before = jnp.where(lane < 64, swapped[:16], swapped[16:32]) - own
    after = jnp.where(lane < 64, swapped[16:32], swapped[32:]) - own
    left = jnp.where(lane % 32 > 0, lanes(own, -1), 0.0) - own
    right = jnp.where(lane % 32 < 31, lanes(own, 1), 0.0) - own
    t0 = jnp.dot(
        jnp.concatenate(split3(own) + split3(before) + split3(after), 0), z_mat[0],
        preferred_element_type=F32,
    ).astype(BF16)
    t1 = jnp.dot(
        jnp.concatenate([jnp.concatenate(split3(left), 0), jnp.concatenate(split3(right), 0)], 1),
        z_mat[1:].reshape(256, 512), preferred_element_type=F32,
    ).astype(BF16)

    def stacked(t, at, column):
        return [
            t[at + 16 * i : at + 16 * i + 16, column + 128 * py : column + 128 * py + 128]
            for i in range(3)
            for py in range(2)
        ]

    for copy, goes, comes in halo:
        pl.when(comes)(copy.wait_recv)
    zero = jnp.zeros((2, 128, 128), F32)

    @pl.when(me == 0)
    def _():
        cells[0:2] = zero

    @pl.when(me == pairs - 1)
    def _():
        cells[10:12] = zero

    for p in (-1, 0, 7, 8):
        chemical(p)

    @pl.when(me == 0)
    def _():
        chem[0] = zero[0]

    @pl.when(me == pairs - 1)
    def _():
        chem[9] = zero[0]

    for f in (0, 1, 6, 7):
        partial(f)

    for px in range(2):
        rhs = jnp.concatenate(stacked(t0, 0, 256 * px) + stacked(t1, 0, 256 * px), 0)
        base = 0.08 * jnp.dot(y_mat[...], rhs, preferred_element_type=F32)
        low = 0.08 * jnp.dot(
            y_mat[:, 96:], jnp.concatenate(stacked(t0, 48, 256 * px), 0), preferred_element_type=F32
        )
        high = 0.08 * jnp.dot(
            y_mat[:, 96:], jnp.concatenate(stacked(t0, 96, 256 * px), 0), preferred_element_type=F32
        )
        out[4 * px] += base + low
        out[4 * px + 1] += base
        out[4 * px + 2] += base
        out[4 * px + 3] += base + high

    done = pltpu.make_async_remote_copy(
        centre.at[pl.ds(0, 15)], pot.at[pl.ds(0, 15)], pot_send, pot_recv,
        device_id=(s, (g + 1) % 16), device_id_type=MESH,
    )
    done.wait_recv()
    done.wait_send()
    lines_in.wait_send()
    for i, there in ((0, above), (1, below)):

        @pl.when(there)
        def _():
            pltpu.make_async_remote_copy(
                lines.at[0:15], lines.at[0:15], cross_send.at[i], cross_recv,
                device_id=(s, (g + 1) % 16), device_id_type=MESH,
            ).wait_send()

    for copy, goes, comes in near + halo:
        pl.when(goes)(copy.wait_send)


def unpack(fine, lines, out, pot, sem):
    copy = pltpu.make_async_copy(fine, out, sem)
    copy.start()
    packed = pot.reshape(64, 32)
    for k in range(4):
        packed[pl.ds(k, 16, stride=4), :] = lines[:, 32 * k : 32 * k + 32]
    copy.wait()


def per_device(comp, guess):
    slabs = lax.axis_size("slab")
    dma = pltpu.SemaphoreType.DMA

    def body(*refs):
        step(slabs, *refs)

    vmem = pl.BlockSpec(memory_space=pltpu.VMEM)
    anywhere = pl.BlockSpec(memory_space=pl.ANY)
    fine, lines = pl.pallas_call(
        body,
        out_shape=(pltpu.VMEM((8, 128, 128), F32), pltpu.VMEM((16, 128), F32)),
        in_specs=[pl.BlockSpec(memory_space=pltpu.HBM)] * 2,
        out_specs=(vmem, vmem),
        scratch_shapes=[
            pltpu.VMEM((12, 128, 128), F32),
            pltpu.VMEM((32, 2, 32), F32),
            pltpu.VMEM((16 + 2 * REACH, 128), F32),
            pltpu.VMEM((WINDOW, 16, 128), F32),
            pltpu.VMEM((WINDOW, 16, 128), F32),
            pltpu.VMEM((WINDOW, 16, 128), F32),
            pltpu.VMEM((10, 128, 128), F32),
            pltpu.VMEM((2, 128, 128), F32),
            pltpu.VMEM((512, 128), BF16),
            pltpu.VMEM((3, 128, 512), BF16),
            pltpu.VMEM((128, 192), BF16),
            pltpu.VMEM((16, 128), F32),
            dma((2,)),
            dma,
            dma,
            dma,
            dma((2,)),
            dma,
            dma((2 * REACH,)),
            dma((2 * REACH,)),
            dma((2,)),
            dma((2,)),
            dma,
            dma,
        ],
        compiler_params=pltpu.CompilerParams(
            collective_id=0, has_side_effects=True, vmem_limit_bytes=62 * 1024 * 1024
        ),
        name="step",
    )(comp, guess)
    return pl.pallas_call(
        unpack,
        out_shape=(jax.ShapeDtypeStruct(comp.shape, F32), jax.ShapeDtypeStruct(guess.shape, F32)),
        in_specs=[vmem, vmem],
        out_specs=(pl.BlockSpec(memory_space=pltpu.HBM), vmem),
        scratch_shapes=[dma],
        compiler_params=pltpu.CompilerParams(vmem_limit_bytes=1024 * 1024),
        name="unpack",
    )(fine, lines)


def solution(mesh):
    placed = (P(("slab", "grp"), None, None), P("slab", "grp", None))
    return jax.shard_map(
        per_device, mesh=mesh, in_specs=placed, out_specs=placed, check_vma=False
    )
```

```python
import jax
import jax.numpy as jnp
from jax import lax
from jax.experimental import pallas as pl
from jax.experimental.pallas import tpu as pltpu
from jax.sharding import PartitionSpec as P

MESH = pl.DeviceIdType.MESH
REACH = 5
WINDOW = 2 * REACH + 1
HUB = 8
FAR_FIRST = (8, 7, 9, 6, 10, 5, 11, 4, 12, 3, 13, 2, 14, 1, 15)
F32 = jnp.float32
BF16 = jnp.bfloat16


def iota(shape, dim):
    return lax.broadcasted_iota(jnp.int32, shape, dim)


def lanes(x, shift):
    return pltpu.roll(x, (-shift) % 128, 1)


def rows(x, shift):
    return pltpu.roll(x, (-shift) % x.shape[0], 0)


def split3(x):
    high = x.astype(BF16)
    rest = x - high.astype(F32)
    mid = rest.astype(BF16)
    low = (rest - mid.astype(F32)).astype(BF16)
    return high, mid, low


def neighbours(v, first, last):
    own = v[16:-16]
    lane, row = iota(own.shape, 1), iota(own.shape, 0) % 16
    a, b = lanes(own, 32), lanes(own, -32)
    up = jnp.where(row < 15, rows(b, 1), 0.0)
    down = jnp.where(row > 0, rows(a, -1), 0.0)
    total = jnp.where(lane % 64 < 32, a + down, b + up)
    total += jnp.where(lane % 32 < 31, lanes(own, 1), 0.0)
    total += jnp.where(lane % 32 > 0, lanes(own, -1), 0.0)
    h = pltpu.roll(v, 64, 1)
    return total + h[16:-16] + jnp.where(lane < 64, h[:-32], h[32:])


def coarse_cycle(source, guess, first_pair, pairs):
    def inside(v, first):
        pair = first_pair + first + iota(v.shape, 0) // 16
        return jnp.where((pair >= 0) & (pair < pairs), v, 0.0)

    def sweep(v, s):
        return 0.2 * v[16:-16] + (0.8 / 6.5) * (s + neighbours(v, 0, 0))

    guess = inside(guess, 0)
    source = inside(source, 0)
    edge = jnp.zeros((16, 128), F32)
    pre = inside(sweep(jnp.concatenate([edge, guess, edge], 0), source), 0)
    resid = inside(source[16:-16] + neighbours(pre, 0, 0) - 6.5 * pre[16:-16], 1)
    lane = iota(resid.shape, 1)
    t = resid + pltpu.roll(resid, 64, 1)
    t = t + jnp.where(lane % 64 < 32, lanes(t, 32), lanes(t, -32))
    t = t + jnp.where(lane % 2 < 1, lanes(t, 1), lanes(t, -1))
    start = t * 0.05
    c, first = start, 1
    for _ in range(2):
        own = c[16:-16]
        lane, row = iota(own.shape, 1) % 32, iota(own.shape, 0) % 16
        total = c[:-32] + c[32:]
        total += jnp.where(row < 15, rows(own, 1), 0.0) + jnp.where(row > 0, rows(own, -1), 0.0)
        total += jnp.where(lane < 30, lanes(own, 2), 0.0) + jnp.where(lane > 1, lanes(own, -2), 0.0)
        first = first + 1
        c = inside(0.2 * own + start[16 * (first - 1) : -16 * (first - 1)] + 0.1 * total, first)
    mid = inside(pre[16 * first : -16 * first] + c, first)
    mid = inside(sweep(mid, source[16 * (first + 1) : -16 * (first + 1)]), first + 1)
    edge = jnp.zeros((16, 128), F32)
    mid = jnp.concatenate([edge, mid, edge], 0)
    return inside(sweep(mid, source[16 * (first + 1) : -16 * (first + 1)]), first + 1)


def plane_neighbours(v):
    row, lane = iota(v.shape, 0), iota(v.shape, 1)
    total = jnp.where(row < 127, rows(v, 1), 0.0) + jnp.where(row > 0, rows(v, -1), 0.0)
    total += jnp.where(lane < 127, lanes(v, 1), 0.0) + jnp.where(lane > 0, lanes(v, -1), 0.0)
    return total


def spread(fine, coarse):
    block, place = fine // 4, fine % 4
    same = jnp.where(block == coarse, 1.0, 0.0)
    first, last = jnp.where(place == 0, 1.0, 0.0), jnp.where(place == 3, 1.0, 0.0)
    second = -same * (first + last)
    second += first * jnp.where(block - 1 == coarse, 1.0, 0.0)
    second += last * jnp.where(block + 1 == coarse, 1.0, 0.0)
    return same, second


def step(
    slabs, comp, guess, out, result, cells, given, lines, sources, guesses, beyond, chem, sums, gather, z_mat,
    y_mat, centre, pot, cell_sem, given_sem, line_send, line_recv, cross_send, cross_recv, near_send, near_recv,
    halo_send, halo_recv, pot_send, pot_recv, word,
):
    s, g = lax.axis_index("slab"), lax.axis_index("grp")
    me = s * 16 + g
    pairs = slabs * 16
    below, above = s > 0, s < slabs - 1
    from_below, from_above = below & (g < REACH), above & (g >= 16 - REACH)
    middle = slabs // 2
    late, early, hub = s == middle - 1, s == middle, (s == middle - 2) & (g == HUB)

    def device(d):
        return (d // 16, d % 16)

    halves = [
        pltpu.make_async_copy(comp.at[4 * h : 4 * h + 4], cells.at[2 + 4 * h : 6 + 4 * h], cell_sem.at[h])
        for h in range(2)
    ]
    load_guess = pltpu.make_async_copy(guess, given, given_sem)
    load_guess.start()
    for half in halves:
        half.start()

    barrier = pltpu.get_barrier_semaphore()
    across = from_below | (from_above & (s != middle - 1) & (s != middle - 2))
    other = jnp.where(g < REACH, s - 1, s + 1)
    for k in FAR_FIRST + (0,):
        peer = (g + k) % 16
        if k:

            @pl.when(jnp.logical_not(late))
            def _():
                pl.semaphore_signal(barrier, 1, device_id=(s, peer), device_id_type=MESH)

        @pl.when(across)
        def _():
            pl.semaphore_signal(barrier, 1, device_id=(other, peer), device_id_type=MESH)

    @pl.when(late)
    def _():
        pl.semaphore_signal(barrier, 1, device_id=(s - 1, HUB), device_id_type=MESH)

    @pl.when(early & (g >= REACH))
    def _():
        for to in range(16 - REACH, 16):
            pl.semaphore_signal(barrier, 1, device_id=(s - 1, to), device_id_type=MESH)

    load_guess.wait()
    packed = given.reshape(64, 32)
    lines[0:REACH] = jnp.zeros((REACH, 128), F32)
    lines[REACH + 16 :] = jnp.zeros((REACH, 128), F32)
    lines[REACH : REACH + 16] = jnp.concatenate(
        [packed[pl.ds(k, 16, stride=4), :] for k in range(4)], axis=1
    )

    def guess_up():
        for to in range(REACH):
            pltpu.make_async_remote_copy(
                lines.at[16 + to : 21], beyond.at[0 : REACH - to, g], cross_send.at[0], cross_recv,
                device_id=(s + 1, to), device_id_type=MESH,
            ).start()

    @pl.when(late)
    def _():
        pl.semaphore_wait(barrier, jnp.where(g < 16 - REACH, REACH, 16))
        guess_up()

        @pl.when(g >= 16 - REACH)
        def _():
            for k in range(16):
                pl.semaphore_signal(
                    word.at[0], 1, device_id=(s + 1, (g + k) % 16), device_id_type=MESH
                )

    at, lane = iota((512, 128), 0), iota((512, 128), 1)
    hit = (at // 128 == lane // 32) & (at % 128 // 4 == lane % 32)
    gather[...] = jnp.where(hit, 1.0 / 64, 0.0).astype(BF16)
    for h in range(2):
        halves[h].wait()
        own = 2 + 4 * h
        sums[h] = (cells[own] + cells[own + 1]) + (cells[own + 2] + cells[own + 3])
    parts = []
    for h in range(2):
        for half in range(2):
            parts.append(sum(sums[h, pl.ds(4 * half + j, 16, stride=8), :] for j in range(4)))
    wide = jnp.concatenate(split3(jnp.concatenate(parts, axis=1)), axis=0)
    means = jnp.dot(wide, gather[...], preferred_element_type=F32)
    sources[REACH] = means[:16] + means[16:32] + means[32:]

    @pl.when(jnp.logical_not(late))
    def _():
        asked = REACH * (above.astype(jnp.int32) + (below & jnp.logical_not(early)).astype(jnp.int32))
        pl.semaphore_wait(barrier, 15 + asked + 16 * hub.astype(jnp.int32))

    @pl.when(hub)
    def _():
        for to in range(16):
            pl.semaphore_signal(word.at[1], 1, device_id=(s + 1, to), device_id_type=MESH)

    pl.when(above & jnp.logical_not(late))(guess_up)

    near = []
    for k in range(REACH, 0, -1):
        for i, o in ((2 * k - 2, k), (2 * k - 1, -k)):
            copy = pltpu.make_async_remote_copy(
                sources.at[REACH], sources.at[REACH - o], near_send.at[i], near_recv.at[i],
                device_id=device(me + o), device_id_type=MESH,
            )
            near.append((copy, o))
    halo = []
    for i, (o, src, dst) in enumerate(((1, comp.at[6:8], cells.at[0:2]), (-1, comp.at[0:2], cells.at[10:12]))):
        copy = pltpu.make_async_remote_copy(
            src, dst, halo_send.at[i], halo_recv.at[i], device_id=device(me + o), device_id_type=MESH
        )
        halo.append((copy, o))

    def goes(o):
        return (me + o >= 0) & (me + o < pairs)

    def comes(o):
        return (me - o >= 0) & (me - o < pairs)

    def guess_down():
        for to in range(16 - REACH, 16):
            pltpu.make_async_remote_copy(
                lines.at[REACH : to - 5], beyond.at[21 - to : WINDOW, g], cross_send.at[1], cross_recv,
                device_id=(s - 1, to), device_id_type=MESH,
            ).start()

    @pl.when(late)
    def _():
        for copy, o in near + halo:
            if o > 0:
                pl.when(g + o > 15)(copy.start)
        pl.semaphore_wait(word.at[1], 1)

    pl.when(below & jnp.logical_not(early))(guess_down)
    for k in FAR_FIRST:
        to = (g + k) % 16
        pltpu.make_async_remote_copy(
            lines.at[pl.ds(to, WINDOW)], guesses.at[:, g], line_send, line_recv,
            device_id=(s, to), device_id_type=MESH,
        ).start()
    guesses[:, pl.ds(g, 1), :] = lines[pl.ds(g, WINDOW), :].reshape(WINDOW, 1, 128)
    for copy, o in near + halo:
        inside = (g + o >= 0) & (g + o < 16)
        rest = jnp.logical_not(late) if o > 0 else jnp.logical_not(early)
        pl.when(inside | (goes(o) & rest))(copy.start)

    @pl.when(early)
    def _():
        pl.semaphore_wait(word.at[0], REACH)
        guess_down()
        for copy, o in near + halo:
            if o < 0:
                pl.when(g + o < 0)(copy.start)

    at, lane = iota((128, 512), 0), iota((128, 512), 1)
    hit = (lane // 128 == at // 32) & (lane % 128 // 4 == at % 32)
    z_mat[0] = jnp.where(hit, 1.0, 0.0).astype(BF16)
    z_mat[1] = jnp.where(hit & (lane % 4 == 0), 1.0, 0.0).astype(BF16)
    z_mat[2] = jnp.where(hit & (lane % 4 == 3), 1.0, 0.0).astype(BF16)
    at, lane = iota((128, 192), 0), iota((128, 192), 1)
    coarse = 2 * (lane % 16) + (lane // 16) % 2
    same, second = spread(at, coarse)
    y_mat[...] = jnp.where(lane < 96, second, same).astype(BF16)

    def chemical(p):
        u = cells[p + 2]
        around = cells[p + 1] + cells[p + 3] + plane_neighbours(u)
        chem[p + 1] = u * u * u + 2.0 * u - 0.5 * around

    def partial(f):
        mu = chem[f + 1]
        around = chem[f] + chem[f + 2] + plane_neighbours(mu)
        out[f] = cells[f + 2] + 0.02 * (around - 6.0 * mu)

    lax.fori_loop(1, 7, lambda p, _: (chemical(p), 0)[1], 0)
    lax.fori_loop(2, 6, lambda f, _: (partial(f), 0)[1], 0)

    lines_in = pltpu.make_async_remote_copy(
        guesses.at[:, 0:15], guesses.at[:, 0:15], line_send, line_recv,
        device_id=(s, (g + 1) % 16), device_id_type=MESH,
    )
    lines_in.wait_recv()
    for there, spots in (
        (from_below, [(j, slice(0, REACH - j)) for j in range(REACH)]),
        (from_above, [(j, slice(21 - j, WINDOW)) for j in range(16 - REACH, 16)]),
    ):
        for j, spot in spots:

            @pl.when(there & (g == j))
            def _():
                pltpu.make_async_remote_copy(
                    beyond.at[spot], beyond.at[spot], cross_send.at[0], cross_recv,
                    device_id=(s, (g + 1) % 16), device_id_type=MESH,
                ).wait_recv()

    for copy, o in near:
        pl.when(comes(o))(copy.wait_recv)
    place = g - REACH + iota((WINDOW * 16, 128), 0) // 16
    start = jnp.where(
        (place >= 0) & (place < 16), guesses[...].reshape(WINDOW * 16, 128), beyond[...].reshape(WINDOW * 16, 128)
    )
    potential = coarse_cycle(sources[...].reshape(WINDOW * 16, 128), start, me - REACH, pairs)
    own = potential[16:32]
    centre[...] = own
    for k in FAR_FIRST:
        to = (g + k) % 16
        pltpu.make_async_remote_copy(
            centre.at[pl.ds(to, 1)], pot.at[pl.ds(g, 1)], pot_send, pot_recv,
            device_id=(s, to), device_id_type=MESH,
        ).start()
    pot[pl.ds(g, 1), :] = centre[pl.ds(g, 1), :]

    lane = iota((16, 128), 1)
    swapped = pltpu.roll(potential, 64, 1)
    before = jnp.where(lane < 64, swapped[:16], swapped[16:32]) - own
    after = jnp.where(lane < 64, swapped[16:32], swapped[32:]) - own
    left = jnp.where(lane % 32 > 0, lanes(own, -1), 0.0) - own
    right = jnp.where(lane % 32 < 31, lanes(own, 1), 0.0) - own
    t0 = jnp.dot(
        jnp.concatenate(split3(own) + split3(before) + split3(after), 0), z_mat[0],
        preferred_element_type=F32,
    ).astype(BF16)
    t1 = jnp.dot(
        jnp.concatenate([jnp.concatenate(split3(left), 0), jnp.concatenate(split3(right), 0)], 1),
        z_mat[1:].reshape(256, 512), preferred_element_type=F32,
    ).astype(BF16)

    def stacked(t, at, column):
        return [
            t[at + 16 * i : at + 16 * i + 16, column + 128 * py : column + 128 * py + 128]
            for i in range(3)
            for py in range(2)
        ]

    for copy, o in halo:
        pl.when(comes(o))(copy.wait_recv)
    zero = jnp.zeros((2, 128, 128), F32)

    @pl.when(me == 0)
    def _():
        cells[0:2] = zero

    @pl.when(me == pairs - 1)
    def _():
        cells[10:12] = zero

    for p in (-1, 0, 7, 8):
        chemical(p)

    @pl.when(me == 0)
    def _():
        chem[0] = zero[0]

    @pl.when(me == pairs - 1)
    def _():
        chem[9] = zero[0]

    for f in (0, 1, 6, 7):
        partial(f)

    for px in range(2):
        rhs = jnp.concatenate(stacked(t0, 0, 256 * px) + stacked(t1, 0, 256 * px), 0)
        base = 0.08 * jnp.dot(y_mat[...], rhs, preferred_element_type=F32)
        low = 0.08 * jnp.dot(
            y_mat[:, 96:], jnp.concatenate(stacked(t0, 48, 256 * px), 0), preferred_element_type=F32
        )
        high = 0.08 * jnp.dot(
            y_mat[:, 96:], jnp.concatenate(stacked(t0, 96, 256 * px), 0), preferred_element_type=F32
        )
        out[4 * px] += base + low
        out[4 * px + 1] += base
        out[4 * px + 2] += base
        out[4 * px + 3] += base + high

    done = pltpu.make_async_remote_copy(
        centre.at[pl.ds(0, 15)], pot.at[pl.ds(0, 15)], pot_send, pot_recv,
        device_id=(s, (g + 1) % 16), device_id_type=MESH,
    )
    done.wait_recv()
    packed = result.reshape(64, 32)
    for k in range(4):
        packed[pl.ds(k, 16, stride=4), :] = pot[:, 32 * k : 32 * k + 32]
    done.wait_send()
    lines_in.wait_send()
    for i, there in ((0, above), (1, below)):

        @pl.when(there)
        def _():
            pltpu.make_async_remote_copy(
                lines.at[0:15], lines.at[0:15], cross_send.at[i], cross_recv,
                device_id=(s, (g + 1) % 16), device_id_type=MESH,
            ).wait_send()

    for copy, o in near + halo:
        pl.when(goes(o))(copy.wait_send)


def deliver(fine, coarse, out, pot, sem):
    copies = [pltpu.make_async_copy(fine, out, sem.at[0]), pltpu.make_async_copy(coarse, pot, sem.at[1])]
    for copy in copies:
        copy.start()
    for copy in copies:
        copy.wait()


def per_device(comp, guess):
    slabs = lax.axis_size("slab")
    dma = pltpu.SemaphoreType.DMA

    def body(*refs):
        step(slabs, *refs)

    vmem = pl.BlockSpec(memory_space=pltpu.VMEM)
    anywhere = pl.BlockSpec(memory_space=pl.ANY)
    fine, lines = pl.pallas_call(
        body,
        out_shape=(pltpu.VMEM((8, 128, 128), F32), pltpu.VMEM((32, 2, 32), F32)),
        in_specs=[pl.BlockSpec(memory_space=pltpu.HBM)] * 2,
        out_specs=(vmem, vmem),
        scratch_shapes=[
            pltpu.VMEM((12, 128, 128), F32),
            pltpu.VMEM((32, 2, 32), F32),
            pltpu.VMEM((16 + 2 * REACH, 128), F32),
            pltpu.VMEM((WINDOW, 16, 128), F32),
            pltpu.VMEM((WINDOW, 16, 128), F32),
            pltpu.VMEM((WINDOW, 16, 128), F32),
            pltpu.VMEM((10, 128, 128), F32),
            pltpu.VMEM((2, 128, 128), F32),
            pltpu.VMEM((512, 128), BF16),
            pltpu.VMEM((3, 128, 512), BF16),
            pltpu.VMEM((128, 192), BF16),
            pltpu.VMEM((16, 128), F32),
            pltpu.VMEM((16, 128), F32),
            dma((2,)),
            dma,
            dma,
            dma,
            dma((2,)),
            dma,
            dma((2 * REACH,)),
            dma((2 * REACH,)),
            dma((2,)),
            dma((2,)),
            dma,
            dma,
            pltpu.SemaphoreType.REGULAR((2,)),
        ],
        compiler_params=pltpu.CompilerParams(
            collective_id=0, has_side_effects=True, vmem_limit_bytes=62 * 1024 * 1024
        ),
        name="step",
    )(comp, guess)
    return pl.pallas_call(
        deliver,
        out_shape=(jax.ShapeDtypeStruct(comp.shape, F32), jax.ShapeDtypeStruct(guess.shape, F32)),
        in_specs=[vmem, vmem],
        out_specs=(pl.BlockSpec(memory_space=pltpu.HBM),) * 2,
        scratch_shapes=[dma((2,))],
        compiler_params=pltpu.CompilerParams(vmem_limit_bytes=1024 * 1024),
        name="deliver",
    )(fine, lines)


def solution(mesh):
    placed = (P(("slab", "grp"), None, None), P("slab", "grp", None))
    return jax.shard_map(
        per_device, mesh=mesh, in_specs=placed, out_specs=placed, check_vma=False
    )
```

```python
import jax
import jax.numpy as jnp
from jax import lax
from jax.experimental import pallas as pl
from jax.experimental.pallas import tpu as pltpu
from jax.sharding import PartitionSpec as P

MESH = pl.DeviceIdType.MESH
REACH = 5
WINDOW = 2 * REACH + 2
UPPER, LOWER = (0, 2, 4), (10, 12, 14)
HUB = 8
FAR_FIRST = (8, 7, 9, 6, 10, 5, 11, 4, 12, 3, 13, 2, 14, 1, 15)
F32 = jnp.float32
BF16 = jnp.bfloat16


def iota(shape, dim):
    return lax.broadcasted_iota(jnp.int32, shape, dim)


def lanes(x, shift):
    return pltpu.roll(x, (-shift) % 128, 1)


def rows(x, shift):
    return pltpu.roll(x, (-shift) % x.shape[0], 0)


def split3(x):
    high = x.astype(BF16)
    rest = x - high.astype(F32)
    mid = rest.astype(BF16)
    low = (rest - mid.astype(F32)).astype(BF16)
    return high, mid, low


def neighbours(v, first, last):
    own = v[16:-16]
    lane, row = iota(own.shape, 1), iota(own.shape, 0) % 16
    a, b = lanes(own, 32), lanes(own, -32)
    up = jnp.where(row < 15, rows(b, 1), 0.0)
    down = jnp.where(row > 0, rows(a, -1), 0.0)
    total = jnp.where(lane % 64 < 32, a + down, b + up)
    total += jnp.where(lane % 32 < 31, lanes(own, 1), 0.0)
    total += jnp.where(lane % 32 > 0, lanes(own, -1), 0.0)
    h = pltpu.roll(v, 64, 1)
    return total + h[16:-16] + jnp.where(lane < 64, h[:-32], h[32:])


def coarse_cycle(source, guess, first_pair, pairs):
    def inside(v, first):
        pair = first_pair + first + iota(v.shape, 0) // 16
        return jnp.where((pair >= 0) & (pair < pairs), v, 0.0)

    def sweep(v, s):
        return 0.2 * v[16:-16] + (0.8 / 6.5) * (s + neighbours(v, 0, 0))

    guess = inside(guess, 0)
    source = inside(source, 0)
    edge = jnp.zeros((16, 128), F32)
    pre = inside(sweep(jnp.concatenate([edge, guess, edge], 0), source), 0)
    resid = inside(source[16:-16] + neighbours(pre, 0, 0) - 6.5 * pre[16:-16], 1)
    lane = iota(resid.shape, 1)
    t = resid + pltpu.roll(resid, 64, 1)
    t = t + jnp.where(lane % 64 < 32, lanes(t, 32), lanes(t, -32))
    t = t + jnp.where(lane % 2 < 1, lanes(t, 1), lanes(t, -1))
    start = t * 0.05
    c, first = start, 1
    for _ in range(2):
        own = c[16:-16]
        lane, row = iota(own.shape, 1) % 32, iota(own.shape, 0) % 16
        total = c[:-32] + c[32:]
        total += jnp.where(row < 15, rows(own, 1), 0.0) + jnp.where(row > 0, rows(own, -1), 0.0)
        total += jnp.where(lane < 30, lanes(own, 2), 0.0) + jnp.where(lane > 1, lanes(own, -2), 0.0)
        first = first + 1
        c = inside(0.2 * own + start[16 * (first - 1) : -16 * (first - 1)] + 0.1 * total, first)
    mid = inside(pre[16 * first : -16 * first] + c, first)
    mid = inside(sweep(mid, source[16 * (first + 1) : -16 * (first + 1)]), first + 1)
    edge = jnp.zeros((16, 128), F32)
    mid = jnp.concatenate([edge, mid, edge], 0)
    return inside(sweep(mid, source[16 * (first + 1) : -16 * (first + 1)]), first + 1)


def plane_neighbours(v):
    row, lane = iota(v.shape, 0), iota(v.shape, 1)
    total = jnp.where(row < 127, rows(v, 1), 0.0) + jnp.where(row > 0, rows(v, -1), 0.0)
    total += jnp.where(lane < 127, lanes(v, 1), 0.0) + jnp.where(lane > 0, lanes(v, -1), 0.0)
    return total


def spread(fine, coarse):
    block, place = fine // 4, fine % 4
    same = jnp.where(block == coarse, 1.0, 0.0)
    first, last = jnp.where(place == 0, 1.0, 0.0), jnp.where(place == 3, 1.0, 0.0)
    second = -same * (first + last)
    second += first * jnp.where(block - 1 == coarse, 1.0, 0.0)
    second += last * jnp.where(block + 1 == coarse, 1.0, 0.0)
    return same, second


def step(
    slabs, comp, guess, out, result, cells, given, lines, sources, guesses, beyond, chem, sums, gather, z_mat,
    y_mat, mine, near_potential, centre, pot, cell_sem, given_sem, line_send, line_recv, cross_send, cross_recv,
    near_send, near_recv, halo_send, halo_recv, pot_send, pot_recv, share_send, share_recv, word,
):
    s, g = lax.axis_index("slab"), lax.axis_index("grp")
    me = s * 16 + g
    pairs = slabs * 16
    below, above = s > 0, s < slabs - 1
    works = g % 2 == 0
    idle = jnp.logical_not(works)
    first = g - g % 2
    middle = slabs // 2
    late, early, hub = s == middle - 1, s == middle, (s == middle - 2) & (g == HUB)
    announce = word.at[0]
    beside = word.at[1]
    down = word.at[2]
    go = word.at[3]

    def device(d):
        return (d // 16, d % 16)

    def tell(semaphore, to):
        pl.semaphore_signal(semaphore, 1, device_id=to, device_id_type=MESH)

    halves = [
        pltpu.make_async_copy(comp.at[4 * h : 4 * h + 4], cells.at[2 + 4 * h : 6 + 4 * h], cell_sem.at[h])
        for h in range(2)
    ]
    load_guess = pltpu.make_async_copy(guess, given, given_sem)
    load_guess.start()
    for half in halves:
        half.start()

    barrier = pltpu.get_barrier_semaphore()

    @pl.when(works & jnp.logical_not(late))
    def _():
        for k in FAR_FIRST:
            tell(barrier, (s, (g + k) % 16))

    @pl.when(works & below & (g < REACH))
    def _():
        for k in FAR_FIRST + (0,):
            tell(barrier, (s - 1, (g + k) % 16))

    @pl.when(works & above & (g >= 16 - WINDOW // 2) & (s != middle - 1) & (s != middle - 2))
    def _():
        for k in FAR_FIRST + (0,):
            tell(barrier, (s + 1, (g + k) % 16))

    @pl.when(late)
    def _():
        tell(barrier, (s - 1, HUB))

    @pl.when(early & (idle | (g >= REACH)))
    def _():
        for to in LOWER:
            tell(barrier, (s - 1, to))

    load_guess.wait()
    packed = given.reshape(64, 32)
    lines[0:REACH] = jnp.zeros((REACH, 128), F32)
    lines[REACH + 16 :] = jnp.zeros((REACH + 1, 128), F32)
    lines[REACH : REACH + 16] = jnp.concatenate(
        [packed[pl.ds(k, 16, stride=4), :] for k in range(4)], axis=1
    )

    def guess_up():
        for to in UPPER:
            pltpu.make_async_remote_copy(
                lines.at[16 + to : 21], beyond.at[0 : REACH - to, g], cross_send.at[0], cross_recv,
                device_id=(s + 1, to), device_id_type=MESH,
            ).start()

    def guess_down():
        for to in LOWER:
            pltpu.make_async_remote_copy(
                lines.at[REACH : to - 4], beyond.at[21 - to : WINDOW, g], cross_send.at[1], cross_recv,
                device_id=(s - 1, to), device_id_type=MESH,
            ).start()

    sends_down = (g == LOWER[0]) | (g == LOWER[1]) | (g == LOWER[2])

    @pl.when(late)
    def _():
        pl.semaphore_wait(barrier, jnp.where(sends_down, 16, 3))
        guess_up()

        @pl.when(sends_down)
        def _():
            for k in range(16):
                tell(down, (s + 1, (g + k) % 16))

        @pl.when(g == 15)
        def _():
            tell(down, (s + 1, 0))

    at, lane = iota((512, 128), 0), iota((512, 128), 1)
    hit = (at // 128 == lane // 32) & (at % 128 // 4 == lane % 32)
    gather[...] = jnp.where(hit, 1.0 / 64, 0.0).astype(BF16)
    for h in range(2):
        halves[h].wait()
        own = 2 + 4 * h
        sums[h] = (cells[own] + cells[own + 1]) + (cells[own + 2] + cells[own + 3])
    parts = []
    for h in range(2):
        for half in range(2):
            parts.append(sum(sums[h, pl.ds(4 * half + j, 16, stride=8), :] for j in range(4)))
    wide = jnp.concatenate(split3(jnp.concatenate(parts, axis=1)), axis=0)
    means = jnp.dot(wide, gather[...], preferred_element_type=F32)
    means = means[:16] + means[16:32] + means[32:]
    mine[...] = means

    @pl.when(works)
    def _():
        sources[REACH] = means

    @pl.when(jnp.logical_not(late))
    def _():
        asked = 3 * (above.astype(jnp.int32) + (below & jnp.logical_not(early)).astype(jnp.int32))
        pl.semaphore_wait(barrier, 7 + g % 2 + asked + 16 * hub.astype(jnp.int32))

    @pl.when(hub)
    def _():
        for to in range(16):
            tell(go, (s + 1, to))

    near = []
    for i in (0, 5, 1, 4, 2, 3):
        o = 2 * i - 6 + g % 2
        copy = pltpu.make_async_remote_copy(
            mine, sources.at[REACH - o], near_send.at[i], near_recv.at[REACH - o],
            device_id=device(me + o), device_id_type=MESH,
        )
        goes = (me + o >= 0) & (me + o < pairs) & (o != 0)
        near.append((copy, o, goes))
    halo = []
    for i, (o, src, dst) in enumerate(((1, comp.at[6:8], cells.at[0:2]), (-1, comp.at[0:2], cells.at[10:12]))):
        copy = pltpu.make_async_remote_copy(
            src, dst, halo_send.at[i], halo_recv.at[i], device_id=device(me + o), device_id_type=MESH
        )
        halo.append((copy, o, (me + o >= 0) & (me + o < pairs)))

    @pl.when(late)
    def _():
        for copy, o, goes in near:
            pl.when(g + o > 15)(copy.start)
        pl.when(g == 15)(halo[0][0].start)
        pl.semaphore_wait(go, 1)

    for j in (4, 3, 5, 2, 6, 1, 7, 0):
        to = (first + 2 * j) % 16
        copy = pltpu.make_async_remote_copy(
            lines.at[pl.ds(to, WINDOW)], guesses.at[:, g], line_send, line_recv,
            device_id=(s, to), device_id_type=MESH,
        )
        if j:
            copy.start()
        else:
            pl.when(idle)(copy.start)
    pl.when(above & jnp.logical_not(late))(guess_up)
    pl.when(below & jnp.logical_not(early))(guess_down)
    for copy, o, goes in near:
        up, under = g + o > 15, g + o < 0
        pl.when(goes & jnp.logical_not((up & late) | (under & early)))(copy.start)

    @pl.when(works)
    def _():
        guesses[:, pl.ds(g, 1), :] = lines[pl.ds(g, WINDOW), :].reshape(WINDOW, 1, 128)
        pl.semaphore_wait(beside, 1 + ((me > 0) & jnp.logical_not(early & (g == 0))).astype(jnp.int32))

    @pl.when(idle)
    def _():
        tell(beside, (s, g - 1))

        @pl.when((me < pairs - 1) & jnp.logical_not(late & (g == 15)))
        def _():
            tell(beside, device(me + 1))

        for j in (4, 3, 5, 2, 6, 1, 7, 0):
            tell(announce, (s, (first + 2 * j) % 16))

    for copy, o, goes in halo:
        apart = late & (g == 15) if o > 0 else early & (g == 0)
        pl.when(goes & jnp.logical_not(apart))(copy.start)

    @pl.when(early)
    def _():
        pl.semaphore_wait(down, 3 + (g == 0).astype(jnp.int32))
        guess_down()
        for copy, o, goes in near:
            pl.when(g + o < 0)(copy.start)
        pl.when(g == 0)(halo[1][0].start)

    at, lane = iota((128, 512), 0), iota((128, 512), 1)
    hit = (lane // 128 == at // 32) & (lane % 128 // 4 == at % 32)
    z_mat[0] = jnp.where(hit, 1.0, 0.0).astype(BF16)
    z_mat[1] = jnp.where(hit & (lane % 4 == 0), 1.0, 0.0).astype(BF16)
    z_mat[2] = jnp.where(hit & (lane % 4 == 3), 1.0, 0.0).astype(BF16)
    at, lane = iota((128, 192), 0), iota((128, 192), 1)
    coarse = 2 * (lane % 16) + (lane // 16) % 2
    same, second = spread(at, coarse)
    y_mat[...] = jnp.where(lane < 96, second, same).astype(BF16)

    def chemical(p):
        u = cells[p + 2]
        around = cells[p + 1] + cells[p + 3] + plane_neighbours(u)
        chem[p + 1] = u * u * u + 2.0 * u - 0.5 * around

    def partial(f):
        mu = chem[f + 1]
        around = chem[f] + chem[f + 2] + plane_neighbours(mu)
        out[f] = cells[f + 2] + 0.02 * (around - 6.0 * mu)

    lax.fori_loop(1, 7, lambda p, _: (chemical(p), 0)[1], 0)
    lax.fori_loop(2, 6, lambda f, _: (partial(f), 0)[1], 0)

    def counted(ref, send, recv):
        return pltpu.make_async_remote_copy(
            ref, ref, send, recv, device_id=(s, (g + 1) % 16), device_id_type=MESH
        )

    share = pltpu.make_async_remote_copy(
        near_potential.at[16:64], near_potential.at[0:48], share_send, share_recv,
        device_id=(s, (g + 1) % 16), device_id_type=MESH,
    )

    @pl.when(works)
    def _():
        counted(guesses.at[:, 0:15], line_send, line_recv).wait_recv()
        for there, spots in (
            (below, [(j, slice(0, REACH - j)) for j in UPPER]),
            (above, [(j, slice(21 - j, WINDOW)) for j in LOWER]),
        ):
            for j, spot in spots:

                @pl.when(there & (g == j))
                def _():
                    counted(beyond.at[spot], cross_send.at[0], cross_recv).wait_recv()

        for k in range(WINDOW):
            if k != REACH:
                comes = (me - REACH + k >= 0) & (me - REACH + k < pairs)
                pl.when(comes)(counted(mine, near_send.at[0], near_recv.at[k]).wait_recv)
        place = g - REACH + iota((WINDOW * 16, 128), 0) // 16
        start = jnp.where(
            (place >= 0) & (place < 16), guesses[...].reshape(WINDOW * 16, 128), beyond[...].reshape(WINDOW * 16, 128)
        )
        potential = coarse_cycle(sources[...].reshape(WINDOW * 16, 128), start, me - REACH, pairs)
        near_potential[...] = potential
        centre[...] = potential[16:48].reshape(2, 16, 128)
        pl.semaphore_wait(announce, 8)
        share.start()
        for k in FAR_FIRST:
            to = (g + k) % 16
            pltpu.make_async_remote_copy(
                centre.at[:, to], pot.at[pl.ds(g, 2)], pot_send, pot_recv,
                device_id=(s, to), device_id_type=MESH,
            ).start()
        pot[pl.ds(g, 2), :] = centre[:, pl.ds(g, 1), :].reshape(2, 128)

    for copy, o, _ in halo:
        pl.when((me - o >= 0) & (me - o < pairs))(copy.wait_recv)
    zero = jnp.zeros((2, 128, 128), F32)

    @pl.when(me == 0)
    def _():
        cells[0:2] = zero

    @pl.when(me == pairs - 1)
    def _():
        cells[10:12] = zero

    for p in (-1, 0, 7, 8):
        chemical(p)

    @pl.when(me == 0)
    def _():
        chem[0] = zero[0]

    @pl.when(me == pairs - 1)
    def _():
        chem[9] = zero[0]

    for f in (0, 1, 6, 7):
        partial(f)

    pl.when(idle)(share.wait_recv)
    potential = near_potential[0:48]
    own = potential[16:32]
    lane = iota((16, 128), 1)
    swapped = pltpu.roll(potential, 64, 1)
    before = jnp.where(lane < 64, swapped[:16], swapped[16:32]) - own
    after = jnp.where(lane < 64, swapped[16:32], swapped[32:]) - own
    left = jnp.where(lane % 32 > 0, lanes(own, -1), 0.0) - own
    right = jnp.where(lane % 32 < 31, lanes(own, 1), 0.0) - own
    t0 = jnp.dot(
        jnp.concatenate(split3(own) + split3(before) + split3(after), 0), z_mat[0],
        preferred_element_type=F32,
    ).astype(BF16)
    t1 = jnp.dot(
        jnp.concatenate([jnp.concatenate(split3(left), 0), jnp.concatenate(split3(right), 0)], 1),
        z_mat[1:].reshape(256, 512), preferred_element_type=F32,
    ).astype(BF16)

    def stacked(t, at, column):
        return [
            t[at + 16 * i : at + 16 * i + 16, column + 128 * py : column + 128 * py + 128]
            for i in range(3)
            for py in range(2)
        ]

    for px in range(2):
        rhs = jnp.concatenate(stacked(t0, 0, 256 * px) + stacked(t1, 0, 256 * px), 0)
        base = 0.08 * jnp.dot(y_mat[...], rhs, preferred_element_type=F32)
        low = 0.08 * jnp.dot(
            y_mat[:, 96:], jnp.concatenate(stacked(t0, 48, 256 * px), 0), preferred_element_type=F32
        )
        high = 0.08 * jnp.dot(
            y_mat[:, 96:], jnp.concatenate(stacked(t0, 96, 256 * px), 0), preferred_element_type=F32
        )
        out[4 * px] += base + low
        out[4 * px + 1] += base
        out[4 * px + 2] += base
        out[4 * px + 3] += base + high

    @pl.when(works)
    def _():
        counted(pot.at[0:14], pot_send, pot_recv).wait_recv()

    @pl.when(idle)
    def _():
        counted(pot.at[0:16], pot_send, pot_recv).wait_recv()

    packed = result.reshape(64, 32)
    for k in range(4):
        packed[pl.ds(k, 16, stride=4), :] = pot[:, 32 * k : 32 * k + 32]

    @pl.when(works)
    def _():
        counted(centre.at[:, 0:15], pot_send, pot_recv).wait_send()
        share.wait_send()
        counted(guesses.at[:, 0:7], line_send, line_recv).wait_send()

    @pl.when(idle)
    def _():
        counted(guesses.at[:, 0:8], line_send, line_recv).wait_send()

    for i, there in ((0, above), (1, below)):

        @pl.when(there)
        def _():
            counted(lines.at[0:9], cross_send.at[i], cross_recv).wait_send()

    for copy, _, goes in near + halo:
        pl.when(goes)(copy.wait_send)


def deliver(fine, coarse, out, pot, sem):
    copies = [pltpu.make_async_copy(fine, out, sem.at[0]), pltpu.make_async_copy(coarse, pot, sem.at[1])]
    for copy in copies:
        copy.start()
    for copy in copies:
        copy.wait()


def per_device(comp, guess):
    slabs = lax.axis_size("slab")
    dma = pltpu.SemaphoreType.DMA

    def body(*refs):
        step(slabs, *refs)

    vmem = pl.BlockSpec(memory_space=pltpu.VMEM)
    anywhere = pl.BlockSpec(memory_space=pl.ANY)
    fine, lines = pl.pallas_call(
        body,
        out_shape=(pltpu.VMEM((8, 128, 128), F32), pltpu.VMEM((32, 2, 32), F32)),
        in_specs=[pl.BlockSpec(memory_space=pltpu.HBM)] * 2,
        out_specs=(vmem, vmem),
        scratch_shapes=[
            pltpu.VMEM((12, 128, 128), F32),
            pltpu.VMEM((32, 2, 32), F32),
            pltpu.VMEM((17 + 2 * REACH, 128), F32),
            pltpu.VMEM((WINDOW, 16, 128), F32),
            pltpu.VMEM((WINDOW, 16, 128), F32),
            pltpu.VMEM((WINDOW, 16, 128), F32),
            pltpu.VMEM((10, 128, 128), F32),
            pltpu.VMEM((2, 128, 128), F32),
            pltpu.VMEM((512, 128), BF16),
            pltpu.VMEM((3, 128, 512), BF16),
            pltpu.VMEM((128, 192), BF16),
            pltpu.VMEM((16, 128), F32),
            pltpu.VMEM((64, 128), F32),
            pltpu.VMEM((2, 16, 128), F32),
            pltpu.VMEM((16, 128), F32),
            dma((2,)),
            dma,
            dma,
            dma,
            dma((2,)),
            dma,
            dma((6,)),
            dma((WINDOW,)),
            dma((2,)),
            dma((2,)),
            dma,
            dma,
            dma,
            dma,
            pltpu.SemaphoreType.REGULAR((4,)),
        ],
        compiler_params=pltpu.CompilerParams(
            collective_id=0, has_side_effects=True, vmem_limit_bytes=62 * 1024 * 1024
        ),
        name="step",
    )(comp, guess)
    return pl.pallas_call(
        deliver,
        out_shape=(jax.ShapeDtypeStruct(comp.shape, F32), jax.ShapeDtypeStruct(guess.shape, F32)),
        in_specs=[vmem, vmem],
        out_specs=(pl.BlockSpec(memory_space=pltpu.HBM),) * 2,
        scratch_shapes=[dma((2,))],
        compiler_params=pltpu.CompilerParams(vmem_limit_bytes=1024 * 1024),
        name="deliver",
    )(fine, lines)


def solution(mesh):
    placed = (P(("slab", "grp"), None, None), P("slab", "grp", None))
    return jax.shard_map(
        per_device, mesh=mesh, in_specs=placed, out_specs=placed, check_vma=False
    )
```

```python
import jax
import jax.numpy as jnp
from jax import lax
from jax.experimental import pallas as pl
from jax.experimental.pallas import tpu as pltpu
from jax.sharding import PartitionSpec as P

MESH = pl.DeviceIdType.MESH
REACH = 5
WINDOW = 2 * REACH + 2
UPPER, LOWER = (0, 2, 4), (10, 12, 14)
HUB = 8
FAR_FIRST = (8, 7, 9, 6, 10, 5, 11, 4, 12, 3, 13, 2, 14, 1, 15)
F32 = jnp.float32
BF16 = jnp.bfloat16


def iota(shape, dim):
    return lax.broadcasted_iota(jnp.int32, shape, dim)


def lanes(x, shift):
    return pltpu.roll(x, (-shift) % 128, 1)


def rows(x, shift):
    return pltpu.roll(x, (-shift) % x.shape[0], 0)


def split3(x):
    high = x.astype(BF16)
    rest = x - high.astype(F32)
    mid = rest.astype(BF16)
    low = (rest - mid.astype(F32)).astype(BF16)
    return high, mid, low


def coarse_cycle(source, guess, first_pair, pairs):
    lane, row = iota((16, 128), 1), iota((16, 128), 0)
    front, odd_row = lane < 64, lane % 64 >= 32
    zero = jnp.zeros((16, 128), F32)
    known = [(first_pair + k >= 0) & (first_pair + k < pairs) for k in range(WINDOW)]
    inside = [jnp.where(k, 1.0, 0.0).astype(F32) for k in known]
    guess = {k: jnp.where(known[k], guess[k], 0.0) for k in guess}
    source = {k: jnp.where(known[k], source[k], 0.0) for k in source}

    def above(v):
        return jnp.where(row < 15, rows(v, 1), 0.0)

    def under(v):
        return jnp.where(row > 0, rows(v, -1), 0.0)

    def neighbours(v, wanted):
        swapped = {k: pltpu.roll(v[k], 64, 1) for k in v}
        done = {}
        for k in wanted:
            line = v[k] + jnp.where(odd_row, under(v[k]), above(v[k]))
            line = jnp.where(odd_row, lanes(line, -32), lanes(line, 32))
            line += jnp.where(lane % 32 < 31, lanes(v[k], 1), 0.0)
            line += jnp.where(lane % 32 > 0, lanes(v[k], -1), 0.0)
            beside = jnp.where(front, swapped.get(k - 1, zero), swapped.get(k + 1, zero))
            done[k] = line + swapped[k] + beside
        return done

    def sweep(v, wanted):
        around = neighbours(v, wanted)
        return {k: inside[k] * (0.2 * v[k] + (0.8 / 6.5) * (source[k] + around[k])) for k in wanted}

    pre = sweep(guess, range(WINDOW))
    places = range(1, WINDOW - 1)
    around = neighbours(pre, places)
    resid = jnp.concatenate(
        [(0.05 * inside[k]) * (source[k] + around[k] - 6.5 * pre[k]) for k in places], 0
    )
    at, to = iota((256, 128), 0), iota((256, 128), 1)
    cell = jnp.where((at % 32) // 2 == (to % 32) // 2, 1.0, 0.0).astype(BF16)
    high, mid, low = split3(resid)
    cells = jnp.dot(jnp.concatenate([high, mid], 1), cell, preferred_element_type=F32)
    cells += jnp.dot(low, cell[:128], preferred_element_type=F32)
    start = {k: cells[16 * (k - 1) : 16 * k] for k in places}
    c = start
    for sweeps in range(1, 3):
        new = {}
        for k in places[sweeps : len(places) - sweeps]:
            v = c[k]
            total = c[k - 1] + c[k + 1] + above(v) + under(v)
            total += jnp.where(lane % 32 < 30, lanes(v, 2), 0.0) + jnp.where(lane % 32 > 1, lanes(v, -2), 0.0)
            new[k] = inside[k] * (0.2 * v + start[k] + 0.1 * total)
        c = new
    v = {k: pre[k] + c[k] for k in c}
    wanted = range(4, WINDOW - 4)
    v = sweep(sweep(v, wanted), wanted)
    return jnp.concatenate([v[k] for k in wanted], 0)


def plane_neighbours(v):
    row, lane = iota(v.shape, 0), iota(v.shape, 1)
    total = jnp.where(row < 127, rows(v, 1), 0.0) + jnp.where(row > 0, rows(v, -1), 0.0)
    total += jnp.where(lane < 127, lanes(v, 1), 0.0) + jnp.where(lane > 0, lanes(v, -1), 0.0)
    return total


def spread(fine, coarse):
    block, place = fine // 4, fine % 4
    same = jnp.where(block == coarse, 1.0, 0.0)
    first, last = jnp.where(place == 0, 1.0, 0.0), jnp.where(place == 3, 1.0, 0.0)
    second = -same * (first + last)
    second += first * jnp.where(block - 1 == coarse, 1.0, 0.0)
    second += last * jnp.where(block + 1 == coarse, 1.0, 0.0)
    return same, second


def step(
    slabs, comp, guess, out, result, cells, given, lines, sources, guesses, beyond, chem, sums, gather, z_mat,
    y_mat, mine, near_potential, centre, pot, cell_sem, given_sem, line_send, line_recv, cross_send, cross_recv,
    near_send, near_recv, halo_send, halo_recv, pot_send, pot_recv, share_send, share_recv, word,
):
    s, g = lax.axis_index("slab"), lax.axis_index("grp")
    me = s * 16 + g
    pairs = slabs * 16
    below, above = s > 0, s < slabs - 1
    works = g % 2 == 0
    idle = jnp.logical_not(works)
    first = g - g % 2
    middle = slabs // 2
    late, early, hub = s == middle - 1, s == middle, (s == middle - 2) & (g == HUB)
    announce = word.at[0]
    beside = word.at[1]
    down = word.at[2]
    go = word.at[3]

    def device(d):
        return (d // 16, d % 16)

    def tell(semaphore, to):
        pl.semaphore_signal(semaphore, 1, device_id=to, device_id_type=MESH)

    halves = [
        pltpu.make_async_copy(comp.at[4 * h : 4 * h + 4], cells.at[2 + 4 * h : 6 + 4 * h], cell_sem.at[h])
        for h in range(2)
    ]
    load_guess = pltpu.make_async_copy(guess, given, given_sem)
    load_guess.start()
    for half in halves:
        half.start()

    barrier = pltpu.get_barrier_semaphore()

    @pl.when(works & jnp.logical_not(late))
    def _():
        for k in FAR_FIRST:
            tell(barrier, (s, (g + k) % 16))

    @pl.when(works & below & (g < REACH))
    def _():
        for k in FAR_FIRST + (0,):
            tell(barrier, (s - 1, (g + k) % 16))

    @pl.when(works & above & (g >= 16 - WINDOW // 2) & (s != middle - 1) & (s != middle - 2))
    def _():
        for k in FAR_FIRST + (0,):
            tell(barrier, (s + 1, (g + k) % 16))

    @pl.when(late)
    def _():
        tell(barrier, (s - 1, HUB))

    @pl.when(early & (idle | (g >= REACH)))
    def _():
        for to in LOWER:
            tell(barrier, (s - 1, to))

    @pl.when(late)
    def _():
        receives = (g == LOWER[0]) | (g == LOWER[1]) | (g == LOWER[2])
        pl.semaphore_wait(barrier, jnp.where(receives, 16, 3))

        @pl.when(receives)
        def _():
            for k in FAR_FIRST + (0,):
                tell(down, (s + 1, (g + k) % 16))

        @pl.when(g == 15)
        def _():
            tell(down, (s + 1, 0))

    lines[0:REACH] = jnp.zeros((REACH, 128), F32)
    lines[REACH + 16 :] = jnp.zeros((REACH + 1, 128), F32)
    at, lane = iota((512, 128), 0), iota((512, 128), 1)
    hit = (at // 128 == lane // 32) & (at % 128 // 4 == lane % 32)
    gather[...] = jnp.where(hit, 1.0 / 64, 0.0).astype(BF16)
    load_guess.wait()
    packed = given.reshape(64, 32)
    lines[REACH : REACH + 16] = jnp.concatenate(
        [packed[pl.ds(k, 16, stride=4), :] for k in range(4)], axis=1
    )

    def guess_up():
        for to in UPPER:
            pltpu.make_async_remote_copy(
                lines.at[16 + to : 21], beyond.at[0 : REACH - to, g], cross_send.at[0], cross_recv,
                device_id=(s + 1, to), device_id_type=MESH,
            ).start()

    def guess_down():
        for to in LOWER:
            pltpu.make_async_remote_copy(
                lines.at[REACH : to - 4], beyond.at[21 - to : WINDOW, g], cross_send.at[1], cross_recv,
                device_id=(s - 1, to), device_id_type=MESH,
            ).start()

    @pl.when(late)
    def _():
        guess_up()

    for h in range(2):
        halves[h].wait()
        own = 2 + 4 * h
        sums[h] = (cells[own] + cells[own + 1]) + (cells[own + 2] + cells[own + 3])
    parts = []
    for h in range(2):
        for half in range(2):
            parts.append(sum(sums[h, pl.ds(4 * half + j, 16, stride=8), :] for j in range(4)))
    wide = jnp.concatenate(split3(jnp.concatenate(parts, axis=1)), axis=0)
    means = jnp.dot(wide, gather[...], preferred_element_type=F32)
    means = means[:16] + means[16:32] + means[32:]
    mine[...] = means

    @pl.when(works)
    def _():
        sources[REACH] = means

    @pl.when(jnp.logical_not(late))
    def _():
        asked = 3 * (above.astype(jnp.int32) + (below & jnp.logical_not(early)).astype(jnp.int32))
        pl.semaphore_wait(barrier, 7 + g % 2 + asked + 16 * hub.astype(jnp.int32))

    @pl.when(hub)
    def _():
        for to in range(16):
            tell(go, (s + 1, to))

    near = []
    for i in (0, 5, 1, 4, 2, 3):
        o = 2 * i - 6 + g % 2
        copy = pltpu.make_async_remote_copy(
            mine, sources.at[REACH - o], near_send.at[i], near_recv,
            device_id=device(me + o), device_id_type=MESH,
        )
        goes = (me + o >= 0) & (me + o < pairs) & (o != 0)
        near.append((copy, o, goes))
    halo = []
    for i, (o, src, dst) in enumerate(((1, comp.at[6:8], cells.at[0:2]), (-1, comp.at[0:2], cells.at[10:12]))):
        copy = pltpu.make_async_remote_copy(
            src, dst, halo_send.at[i], halo_recv.at[i], device_id=device(me + o), device_id_type=MESH
        )
        halo.append((copy, o, (me + o >= 0) & (me + o < pairs)))

    @pl.when(late)
    def _():
        for copy, o, goes in near:
            pl.when(g + o > 15)(copy.start)
        pl.when(g == 15)(halo[0][0].start)
        pl.semaphore_wait(go, 1)

    pl.when(above & jnp.logical_not(late))(guess_up)
    pl.when(below & jnp.logical_not(early))(guess_down)
    for j in (4, 3, 5, 2, 6, 1, 7, 0):
        to = (first + 2 * j) % 16
        copy = pltpu.make_async_remote_copy(
            lines.at[pl.ds(to, WINDOW)], guesses.at[:, g], line_send, line_recv,
            device_id=(s, to), device_id_type=MESH,
        )
        if j:
            copy.start()
        else:
            pl.when(idle)(copy.start)
    for copy, o, goes in near:
        up, under = g + o > 15, g + o < 0
        pl.when(goes & jnp.logical_not((up & late) | (under & early)))(copy.start)

    @pl.when(works)
    def _():
        guesses[:, pl.ds(g, 1), :] = lines[pl.ds(g, WINDOW), :].reshape(WINDOW, 1, 128)
        pl.semaphore_wait(beside, 1 + ((me > 0) & jnp.logical_not(early & (g == 0))).astype(jnp.int32))

    @pl.when(idle)
    def _():
        tell(beside, (s, g - 1))

        @pl.when((me < pairs - 1) & jnp.logical_not(late & (g == 15)))
        def _():
            tell(beside, device(me + 1))

        for j in (4, 3, 5, 2, 6, 1, 7, 0):
            tell(announce, (s, (first + 2 * j) % 16))

    for copy, o, goes in halo:
        apart = late & (g == 15) if o > 0 else early & (g == 0)
        pl.when(goes & jnp.logical_not(apart))(copy.start)

    @pl.when(early)
    def _():
        pl.semaphore_wait(down, 3 + (g == 0).astype(jnp.int32))
        guess_down()
        for copy, o, goes in near:
            pl.when(g + o < 0)(copy.start)
        pl.when(g == 0)(halo[1][0].start)

    at, lane = iota((128, 512), 0), iota((128, 512), 1)
    hit = (lane // 128 == at // 32) & (lane % 128 // 4 == at % 32)
    z_mat[0] = jnp.where(hit, 1.0, 0.0).astype(BF16)
    z_mat[1] = jnp.where(hit & (lane % 4 == 0), 1.0, 0.0).astype(BF16)
    z_mat[2] = jnp.where(hit & (lane % 4 == 3), 1.0, 0.0).astype(BF16)
    at, lane = iota((128, 192), 0), iota((128, 192), 1)
    coarse = 2 * (lane % 16) + (lane // 16) % 2
    same, second = spread(at, coarse)
    y_mat[...] = jnp.where(lane < 96, second, same).astype(BF16)

    def chemical(p):
        u = cells[p + 2]
        around = cells[p + 1] + cells[p + 3] + plane_neighbours(u)
        chem[p + 1] = u * u * u + 2.0 * u - 0.5 * around

    def partial(f):
        mu = chem[f + 1]
        around = chem[f] + chem[f + 2] + plane_neighbours(mu)
        out[f] = cells[f + 2] + 0.02 * (around - 6.0 * mu)

    lax.fori_loop(1, 7, lambda p, _: (chemical(p), 0)[1], 0)
    lax.fori_loop(2, 6, lambda f, _: (partial(f), 0)[1], 0)

    def counted(ref, send, recv):
        return pltpu.make_async_remote_copy(
            ref, ref, send, recv, device_id=(s, (g + 1) % 16), device_id_type=MESH
        )

    share = pltpu.make_async_remote_copy(
        near_potential.at[16:64], near_potential.at[0:48], share_send, share_recv,
        device_id=(s, (g + 1) % 16), device_id_type=MESH,
    )

    @pl.when(works)
    def _():
        counted(guesses.at[:, 0:15], line_send, line_recv).wait_recv()
        for there, spots in (
            (below, [(j, slice(0, REACH - j)) for j in UPPER]),
            (above, [(j, slice(21 - j, WINDOW)) for j in LOWER]),
        ):
            for j, spot in spots:

                @pl.when(there & (g == j))
                def _():
                    counted(beyond.at[spot], cross_send.at[0], cross_recv).wait_recv()

        lost = jnp.maximum(REACH - me, 0) + jnp.maximum(me + 7 - pairs, 0)
        for less in (0, 1, 3, 5):

            @pl.when(lost == less)
            def _():
                counted(sources.at[0 : WINDOW - 1 - less], near_send.at[0], near_recv).wait_recv()

        start = {
            k: jnp.where((g - REACH + k >= 0) & (g - REACH + k < 16), guesses[k], beyond[k]) for k in range(WINDOW)
        }
        potential = coarse_cycle({k: sources[k] for k in range(WINDOW)}, start, me - REACH, pairs)
        near_potential[...] = potential
        centre[...] = potential[16:48].reshape(2, 16, 128)
        pl.semaphore_wait(announce, 8)
        share.start()
        for k in FAR_FIRST:
            to = (g + k) % 16
            pltpu.make_async_remote_copy(
                centre.at[:, to], pot.at[pl.ds(g, 2)], pot_send, pot_recv,
                device_id=(s, to), device_id_type=MESH,
            ).start()
        pot[pl.ds(g, 2), :] = centre[:, pl.ds(g, 1), :].reshape(2, 128)

    for copy, o, _ in halo:
        pl.when((me - o >= 0) & (me - o < pairs))(copy.wait_recv)
    zero = jnp.zeros((2, 128, 128), F32)

    @pl.when(me == 0)
    def _():
        cells[0:2] = zero

    @pl.when(me == pairs - 1)
    def _():
        cells[10:12] = zero

    for p in (-1, 0, 7, 8):
        chemical(p)

    @pl.when(me == 0)
    def _():
        chem[0] = zero[0]

    @pl.when(me == pairs - 1)
    def _():
        chem[9] = zero[0]

    for f in (0, 1, 6, 7):
        partial(f)

    pl.when(idle)(share.wait_recv)
    potential = near_potential[0:48]
    own = potential[16:32]
    lane = iota((16, 128), 1)
    swapped = pltpu.roll(potential, 64, 1)
    before = jnp.where(lane < 64, swapped[:16], swapped[16:32]) - own
    after = jnp.where(lane < 64, swapped[16:32], swapped[32:]) - own
    left = jnp.where(lane % 32 > 0, lanes(own, -1), 0.0) - own
    right = jnp.where(lane % 32 < 31, lanes(own, 1), 0.0) - own
    t0 = jnp.dot(
        jnp.concatenate(split3(own) + split3(before) + split3(after), 0), z_mat[0],
        preferred_element_type=F32,
    ).astype(BF16)
    t1 = jnp.dot(
        jnp.concatenate([jnp.concatenate(split3(left), 0), jnp.concatenate(split3(right), 0)], 1),
        z_mat[1:].reshape(256, 512), preferred_element_type=F32,
    ).astype(BF16)

    def stacked(t, at, column):
        return [
            t[at + 16 * i : at + 16 * i + 16, column + 128 * py : column + 128 * py + 128]
            for i in range(3)
            for py in range(2)
        ]

    for px in range(2):
        rhs = jnp.concatenate(stacked(t0, 0, 256 * px) + stacked(t1, 0, 256 * px), 0)
        base = 0.08 * jnp.dot(y_mat[...], rhs, preferred_element_type=F32)
        low = 0.08 * jnp.dot(
            y_mat[:, 96:], jnp.concatenate(stacked(t0, 48, 256 * px), 0), preferred_element_type=F32
        )
        high = 0.08 * jnp.dot(
            y_mat[:, 96:], jnp.concatenate(stacked(t0, 96, 256 * px), 0), preferred_element_type=F32
        )
        out[4 * px] += base + low
        out[4 * px + 1] += base
        out[4 * px + 2] += base
        out[4 * px + 3] += base + high

    @pl.when(works)
    def _():
        counted(guesses.at[:, 0:7], line_send, line_recv).wait_send()

    @pl.when(idle)
    def _():
        counted(guesses.at[:, 0:8], line_send, line_recv).wait_send()

    for i, there in ((0, above), (1, below)):

        @pl.when(there)
        def _():
            counted(lines.at[0:9], cross_send.at[i], cross_recv).wait_send()

    for copy, _, goes in near + halo:
        pl.when(goes)(copy.wait_send)

    @pl.when(works)
    def _():
        share.wait_send()
        counted(centre.at[:, 0:15], pot_send, pot_recv).wait_send()
        counted(pot.at[0:14], pot_send, pot_recv).wait_recv()

    @pl.when(idle)
    def _():
        counted(pot.at[0:16], pot_send, pot_recv).wait_recv()

    packed = result.reshape(64, 32)
    for k in range(4):
        packed[pl.ds(k, 16, stride=4), :] = pot[:, 32 * k : 32 * k + 32]


def deliver(fine, coarse, out, pot, sem):
    copies = [pltpu.make_async_copy(fine, out, sem.at[0]), pltpu.make_async_copy(coarse, pot, sem.at[1])]
    for copy in copies:
        copy.start()
    for copy in copies:
        copy.wait()


def per_device(comp, guess):
    slabs = lax.axis_size("slab")
    dma = pltpu.SemaphoreType.DMA

    def body(*refs):
        step(slabs, *refs)

    vmem = pl.BlockSpec(memory_space=pltpu.VMEM)
    anywhere = pl.BlockSpec(memory_space=pl.ANY)
    fine, lines = pl.pallas_call(
        body,
        out_shape=(pltpu.VMEM((8, 128, 128), F32), pltpu.VMEM((32, 2, 32), F32)),
        in_specs=[pl.BlockSpec(memory_space=pltpu.HBM)] * 2,
        out_specs=(vmem, vmem),
        scratch_shapes=[
            pltpu.VMEM((12, 128, 128), F32),
            pltpu.VMEM((32, 2, 32), F32),
            pltpu.VMEM((17 + 2 * REACH, 128), F32),
            pltpu.VMEM((WINDOW, 16, 128), F32),
            pltpu.VMEM((WINDOW, 16, 128), F32),
            pltpu.VMEM((WINDOW, 16, 128), F32),
            pltpu.VMEM((10, 128, 128), F32),
            pltpu.VMEM((2, 128, 128), F32),
            pltpu.VMEM((512, 128), BF16),
            pltpu.VMEM((3, 128, 512), BF16),
            pltpu.VMEM((128, 192), BF16),
            pltpu.VMEM((16, 128), F32),
            pltpu.VMEM((64, 128), F32),
            pltpu.VMEM((2, 16, 128), F32),
            pltpu.VMEM((16, 128), F32),
            dma((2,)),
            dma,
            dma,
            dma,
            dma((2,)),
            dma,
            dma((6,)),
            dma,
            dma((2,)),
            dma((2,)),
            dma,
            dma,
            dma,
            dma,
            pltpu.SemaphoreType.REGULAR((4,)),
        ],
        compiler_params=pltpu.CompilerParams(
            collective_id=0, has_side_effects=True, vmem_limit_bytes=62 * 1024 * 1024
        ),
        name="step",
    )(comp, guess)
    return pl.pallas_call(
        deliver,
        out_shape=(jax.ShapeDtypeStruct(comp.shape, F32), jax.ShapeDtypeStruct(guess.shape, F32)),
        in_specs=[vmem, vmem],
        out_specs=(pl.BlockSpec(memory_space=pltpu.HBM),) * 2,
        scratch_shapes=[dma((2,))],
        compiler_params=pltpu.CompilerParams(vmem_limit_bytes=1024 * 1024),
        name="deliver",
    )(fine, lines)


def solution(mesh):
    placed = (P(("slab", "grp"), None, None), P("slab", "grp", None))
    return jax.shard_map(
        per_device, mesh=mesh, in_specs=placed, out_specs=placed, check_vma=False
    )
```

```python
import jax
import jax.numpy as jnp
from jax import lax
from jax.experimental import pallas as pl
from jax.experimental.pallas import tpu as pltpu
from jax.sharding import PartitionSpec as P

MESH = pl.DeviceIdType.MESH
REACH = 5
WINDOW = 2 * REACH + 2
UPPER, LOWER = (0, 2, 4), (10, 12, 14)
HUB = 8
FAR_FIRST = (8, 7, 9, 6, 10, 5, 11, 4, 12, 3, 13, 2, 14, 1, 15)
F32 = jnp.float32
BF16 = jnp.bfloat16


def iota(shape, dim):
    return lax.broadcasted_iota(jnp.int32, shape, dim)


def lanes(x, shift):
    return pltpu.roll(x, (-shift) % 128, 1)


def rows(x, shift):
    return pltpu.roll(x, (-shift) % x.shape[0], 0)


def split3(x):
    high = x.astype(BF16)
    rest = x - high.astype(F32)
    mid = rest.astype(BF16)
    low = (rest - mid.astype(F32)).astype(BF16)
    return high, mid, low


def coarse_cycle(source, guess, first_pair, pairs):
    lane, row = iota((16, 128), 1), iota((16, 128), 0)
    front, odd_row = lane < 64, lane % 64 >= 32
    zero = jnp.zeros((16, 128), F32)
    known = [(first_pair + k >= 0) & (first_pair + k < pairs) for k in range(WINDOW)]
    inside = [jnp.where(k, 1.0, 0.0).astype(F32) for k in known]
    guess = {k: jnp.where(known[k], guess[k], 0.0) for k in guess}
    source = {k: jnp.where(known[k], source[k], 0.0) for k in source}

    def above(v):
        return jnp.where(row < 15, rows(v, 1), 0.0)

    def under(v):
        return jnp.where(row > 0, rows(v, -1), 0.0)

    def neighbours(v, wanted):
        swapped = {k: pltpu.roll(v[k], 64, 1) for k in v}
        done = {}
        for k in wanted:
            line = v[k] + jnp.where(odd_row, under(v[k]), above(v[k]))
            line = jnp.where(odd_row, lanes(line, -32), lanes(line, 32))
            line += jnp.where(lane % 32 < 31, lanes(v[k], 1), 0.0)
            line += jnp.where(lane % 32 > 0, lanes(v[k], -1), 0.0)
            beside = jnp.where(front, swapped.get(k - 1, zero), swapped.get(k + 1, zero))
            done[k] = line + swapped[k] + beside
        return done

    def sweep(v, wanted):
        around = neighbours(v, wanted)
        return {k: inside[k] * (0.2 * v[k] + (0.8 / 6.5) * (source[k] + around[k])) for k in wanted}

    pre = sweep(guess, range(WINDOW))
    places = range(1, WINDOW - 1)
    around = neighbours(pre, places)
    resid = jnp.concatenate(
        [(0.05 * inside[k]) * (source[k] + around[k] - 6.5 * pre[k]) for k in places], 0
    )
    at, to = iota((256, 128), 0), iota((256, 128), 1)
    cell = jnp.where((at % 32) // 2 == (to % 32) // 2, 1.0, 0.0).astype(BF16)
    high, mid, low = split3(resid)
    cells = jnp.dot(jnp.concatenate([high, mid], 1), cell, preferred_element_type=F32)
    cells += jnp.dot(low, cell[:128], preferred_element_type=F32)
    start = {k: cells[16 * (k - 1) : 16 * k] for k in places}
    c = start
    for sweeps in range(1, 3):
        new = {}
        for k in places[sweeps : len(places) - sweeps]:
            v = c[k]
            total = c[k - 1] + c[k + 1] + above(v) + under(v)
            total += jnp.where(lane % 32 < 30, lanes(v, 2), 0.0) + jnp.where(lane % 32 > 1, lanes(v, -2), 0.0)
            new[k] = inside[k] * (0.2 * v + start[k] + 0.1 * total)
        c = new
    v = {k: pre[k] + c[k] for k in c}
    wanted = range(4, WINDOW - 4)
    v = sweep(sweep(v, wanted), wanted)
    return jnp.concatenate([v[k] for k in wanted], 0)


def plane_neighbours(v):
    row, lane = iota(v.shape, 0), iota(v.shape, 1)
    total = jnp.where(row < 127, rows(v, 1), 0.0) + jnp.where(row > 0, rows(v, -1), 0.0)
    total += jnp.where(lane < 127, lanes(v, 1), 0.0) + jnp.where(lane > 0, lanes(v, -1), 0.0)
    return total


def spread(fine, coarse):
    block, place = fine // 4, fine % 4
    same = jnp.where(block == coarse, 1.0, 0.0)
    first, last = jnp.where(place == 0, 1.0, 0.0), jnp.where(place == 3, 1.0, 0.0)
    second = -same * (first + last)
    second += first * jnp.where(block - 1 == coarse, 1.0, 0.0)
    second += last * jnp.where(block + 1 == coarse, 1.0, 0.0)
    return same, second


def step(
    slabs, comp, guess, out, result, cells, given, lines, sources, guesses, beyond, chem, sums, gather, z_mat,
    y_mat, mine, near_potential, centre, pot, cell_sem, given_sem, line_send, line_recv, cross_send, cross_recv,
    near_send, near_recv, halo_send, halo_recv, pot_send, pot_recv, share_send, share_recv, word,
):
    s, g = lax.axis_index("slab"), lax.axis_index("grp")
    me = s * 16 + g
    pairs = slabs * 16
    below, above = s > 0, s < slabs - 1
    first = g - g % 2
    second = (s == 0) & (first == 0)
    works = jnp.where(second, g == 1, g == first)
    idle = jnp.logical_not(works)
    base = s * 16 + first
    middle = slabs // 2
    late, early, hub = s == middle - 1, s == middle, (s == middle - 2) & (g == HUB)
    announce = word.at[0]
    beside = word.at[1]
    down = word.at[2]
    go = word.at[3]

    def device(d):
        return (d // 16, d % 16)

    def worker(pair):
        return device(jnp.where(pair == 0, 1, pair))

    def tell(semaphore, to):
        pl.semaphore_signal(semaphore, 1, device_id=to, device_id_type=MESH)

    halves = [
        pltpu.make_async_copy(comp.at[4 * h : 4 * h + 4], cells.at[2 + 4 * h : 6 + 4 * h], cell_sem.at[h])
        for h in range(2)
    ]
    load_guess = pltpu.make_async_copy(guess, given, given_sem)
    load_guess.start()
    for half in halves:
        half.start()

    barrier = pltpu.get_barrier_semaphore()

    @pl.when(works & jnp.logical_not(late))
    def _():
        for k in FAR_FIRST:
            tell(barrier, (s, (g + k) % 16))

    @pl.when(works & below & (g < REACH))
    def _():
        for k in FAR_FIRST + (0,):
            tell(barrier, (s - 1, (g + k) % 16))

    @pl.when(works & above & (g >= 16 - WINDOW // 2) & (s != middle - 1) & (s != middle - 2))
    def _():
        for k in FAR_FIRST + (0,):
            tell(barrier, (s + 1, (g + k) % 16))

    @pl.when(late)
    def _():
        tell(barrier, (s - 1, HUB))

    @pl.when(early & (idle | (g >= REACH)))
    def _():
        for to in LOWER:
            tell(barrier, (s - 1, to))

    @pl.when(late)
    def _():
        receives = (g == LOWER[0]) | (g == LOWER[1]) | (g == LOWER[2])
        pl.semaphore_wait(barrier, jnp.where(receives, 16, 3))

        @pl.when(receives)
        def _():
            for k in FAR_FIRST + (0,):
                tell(down, (s + 1, (g + k) % 16))

        @pl.when(g == 15)
        def _():
            tell(down, (s + 1, 0))

    lines[0:REACH] = jnp.zeros((REACH, 128), F32)
    lines[REACH + 16 :] = jnp.zeros((REACH + 1, 128), F32)
    at, lane = iota((512, 128), 0), iota((512, 128), 1)
    hit = (at // 128 == lane // 32) & (at % 128 // 4 == lane % 32)
    gather[...] = jnp.where(hit, 1.0 / 64, 0.0).astype(BF16)
    load_guess.wait()
    packed = given.reshape(64, 32)
    lines[REACH : REACH + 16] = jnp.concatenate(
        [packed[pl.ds(k, 16, stride=4), :] for k in range(4)], axis=1
    )

    def guess_up():
        for to in UPPER:
            pltpu.make_async_remote_copy(
                lines.at[16 + to : 21], beyond.at[0 : REACH - to, g], cross_send.at[0], cross_recv,
                device_id=(s + 1, to), device_id_type=MESH,
            ).start()

    def guess_down():
        for to in LOWER:
            pltpu.make_async_remote_copy(
                lines.at[REACH : to - 4], beyond.at[21 - to : WINDOW, g], cross_send.at[1], cross_recv,
                device_id=(s - 1, to), device_id_type=MESH,
            ).start()

    @pl.when(late)
    def _():
        guess_up()

    for h in range(2):
        halves[h].wait()
        own = 2 + 4 * h
        sums[h] = (cells[own] + cells[own + 1]) + (cells[own + 2] + cells[own + 3])
    parts = []
    for h in range(2):
        for half in range(2):
            parts.append(sum(sums[h, pl.ds(4 * half + j, 16, stride=8), :] for j in range(4)))
    wide = jnp.concatenate(split3(jnp.concatenate(parts, axis=1)), axis=0)
    means = jnp.dot(wide, gather[...], preferred_element_type=F32)
    means = means[:16] + means[16:32] + means[32:]
    mine[...] = means

    @pl.when(works)
    def _():
        sources[REACH + g - first] = means

    @pl.when(jnp.logical_not(late))
    def _():
        asked = 3 * (above.astype(jnp.int32) + (below & jnp.logical_not(early)).astype(jnp.int32))
        pl.semaphore_wait(barrier, 7 + idle.astype(jnp.int32) + asked + 16 * hub.astype(jnp.int32))

    @pl.when(hub)
    def _():
        for to in range(16):
            tell(go, (s + 1, to))

    near = []
    for i in (0, 5, 1, 4, 2, 3):
        o = 2 * i - 6 + g % 2
        copy = pltpu.make_async_remote_copy(
            mine, sources.at[REACH - o], near_send.at[i], near_recv,
            device_id=worker(me + o), device_id_type=MESH,
        )
        itself = works & (me + o == base)
        goes = (me + o >= 0) & (me + o < pairs) & jnp.logical_not(itself)
        near.append((copy, o, goes))
    halo = []
    for i, (o, src, dst) in enumerate(((1, comp.at[6:8], cells.at[0:2]), (-1, comp.at[0:2], cells.at[10:12]))):
        copy = pltpu.make_async_remote_copy(
            src, dst, halo_send.at[i], halo_recv.at[i], device_id=device(me + o), device_id_type=MESH
        )
        halo.append((copy, o, (me + o >= 0) & (me + o < pairs)))

    @pl.when(late)
    def _():
        for copy, o, goes in near:
            pl.when(g + o > 15)(copy.start)
        pl.when(g == 15)(halo[0][0].start)
        pl.semaphore_wait(go, 1)

    pl.when(above & jnp.logical_not(late))(guess_up)
    pl.when(below & jnp.logical_not(early))(guess_down)
    for j in (4, 3, 5, 2, 6, 1, 7, 0):
        to = (first + 2 * j) % 16
        copy = pltpu.make_async_remote_copy(
            lines.at[pl.ds(to, WINDOW)], guesses.at[:, g], line_send, line_recv,
            device_id=worker(s * 16 + to), device_id_type=MESH,
        )
        if j:
            copy.start()
        else:
            pl.when(idle)(copy.start)
    for copy, o, goes in near:
        up, under = g + o > 15, g + o < 0
        pl.when(goes & jnp.logical_not((up & late) | (under & early)))(copy.start)

    @pl.when(works)
    def _():
        guesses[:, pl.ds(g, 1), :] = lines[pl.ds(first, WINDOW), :].reshape(WINDOW, 1, 128)
        alone = (early & (g == 0)) | ((s == 0) & ((g == 1) | (g == 2)))
        pl.semaphore_wait(beside, jnp.where(alone, 1, 2))

    @pl.when(idle)
    def _():
        @pl.when(g > 0)
        def _():
            tell(beside, (s, g - 1))

        @pl.when((me < pairs - 1) & jnp.logical_not(late & (g == 15)))
        def _():
            tell(beside, device(me + 1))

        for j in (4, 3, 5, 2, 6, 1, 7, 0):
            tell(announce, worker(s * 16 + (first + 2 * j) % 16))

    for copy, o, goes in halo:
        apart = late & (g == 15) if o > 0 else early & (g == 0)
        pl.when(goes & jnp.logical_not(apart))(copy.start)

    @pl.when(early)
    def _():
        pl.semaphore_wait(down, 3 + (g == 0).astype(jnp.int32))
        guess_down()
        for copy, o, goes in near:
            pl.when(g + o < 0)(copy.start)
        pl.when(g == 0)(halo[1][0].start)

    at, lane = iota((128, 512), 0), iota((128, 512), 1)
    hit = (lane // 128 == at // 32) & (lane % 128 // 4 == at % 32)
    z_mat[0] = jnp.where(hit, 1.0, 0.0).astype(BF16)
    z_mat[1] = jnp.where(hit & (lane % 4 == 0), 1.0, 0.0).astype(BF16)
    z_mat[2] = jnp.where(hit & (lane % 4 == 3), 1.0, 0.0).astype(BF16)
    at, lane = iota((128, 192), 0), iota((128, 192), 1)
    coarse = 2 * (lane % 16) + (lane // 16) % 2
    same, second = spread(at, coarse)
    y_mat[...] = jnp.where(lane < 96, second, same).astype(BF16)

    def chemical(p):
        u = cells[p + 2]
        around = cells[p + 1] + cells[p + 3] + plane_neighbours(u)
        chem[p + 1] = u * u * u + 2.0 * u - 0.5 * around

    def partial(f):
        mu = chem[f + 1]
        around = chem[f] + chem[f + 2] + plane_neighbours(mu)
        out[f] = cells[f + 2] + 0.02 * (around - 6.0 * mu)

    lax.fori_loop(1, 7, lambda p, _: (chemical(p), 0)[1], 0)
    lax.fori_loop(2, 6, lambda f, _: (partial(f), 0)[1], 0)

    def counted(ref, send, recv):
        return pltpu.make_async_remote_copy(
            ref, ref, send, recv, device_id=(s, (g + 1) % 16), device_id_type=MESH
        )

    share = pltpu.make_async_remote_copy(
        near_potential.at[pl.ds(16 * (1 + first - g), 48)], near_potential.at[0:48], share_send, share_recv,
        device_id=(s, 2 * first + 1 - g), device_id_type=MESH,
    )

    @pl.when(works)
    def _():
        counted(guesses.at[:, 0:15], line_send, line_recv).wait_recv()
        for there, spots in (
            (below, [(j, slice(0, REACH - j)) for j in UPPER]),
            (above, [(j, slice(21 - j, WINDOW)) for j in LOWER]),
        ):
            for j, spot in spots:

                @pl.when(there & (g == j))
                def _():
                    counted(beyond.at[spot], cross_send.at[0], cross_recv).wait_recv()

        lost = jnp.maximum(REACH - base, 0) + jnp.maximum(base + 7 - pairs, 0)
        for less in (0, 1, 3, 5):

            @pl.when(lost == less)
            def _():
                counted(sources.at[0 : WINDOW - 1 - less], near_send.at[0], near_recv).wait_recv()

        start = {
            k: jnp.where((first - REACH + k >= 0) & (first - REACH + k < 16), guesses[k], beyond[k]) for k in range(WINDOW)
        }
        potential = coarse_cycle({k: sources[k] for k in range(WINDOW)}, start, base - REACH, pairs)
        near_potential[...] = potential
        centre[...] = potential[16:48].reshape(2, 16, 128)
        pl.semaphore_wait(announce, 8)
        share.start()
        for k in FAR_FIRST:
            to = (g + k) % 16
            pltpu.make_async_remote_copy(
                centre.at[:, to], pot.at[pl.ds(first, 2)], pot_send, pot_recv,
                device_id=(s, to), device_id_type=MESH,
            ).start()
        pot[pl.ds(first, 2), :] = centre[:, pl.ds(g, 1), :].reshape(2, 128)

    for copy, o, _ in halo:
        pl.when((me - o >= 0) & (me - o < pairs))(copy.wait_recv)
    zero = jnp.zeros((2, 128, 128), F32)

    @pl.when(me == 0)
    def _():
        cells[0:2] = zero

    @pl.when(me == pairs - 1)
    def _():
        cells[10:12] = zero

    for p in (-1, 0, 7, 8):
        chemical(p)

    @pl.when(me == 0)
    def _():
        chem[0] = zero[0]

    @pl.when(me == pairs - 1)
    def _():
        chem[9] = zero[0]

    for f in (0, 1, 6, 7):
        partial(f)

    pl.when(idle)(share.wait_recv)
    potential = near_potential[pl.ds(jnp.where(works, 16 * (g - first), 0), 48), :]
    own = potential[16:32]
    lane = iota((16, 128), 1)
    swapped = pltpu.roll(potential, 64, 1)
    before = jnp.where(lane < 64, swapped[:16], swapped[16:32]) - own
    after = jnp.where(lane < 64, swapped[16:32], swapped[32:]) - own
    left = jnp.where(lane % 32 > 0, lanes(own, -1), 0.0) - own
    right = jnp.where(lane % 32 < 31, lanes(own, 1), 0.0) - own
    t0 = jnp.dot(
        jnp.concatenate(split3(own) + split3(before) + split3(after), 0), z_mat[0],
        preferred_element_type=F32,
    ).astype(BF16)
    t1 = jnp.dot(
        jnp.concatenate([jnp.concatenate(split3(left), 0), jnp.concatenate(split3(right), 0)], 1),
        z_mat[1:].reshape(256, 512), preferred_element_type=F32,
    ).astype(BF16)

    def stacked(t, at, column):
        return [
            t[at + 16 * i : at + 16 * i + 16, column + 128 * py : column + 128 * py + 128]
            for i in range(3)
            for py in range(2)
        ]

    for px in range(2):
        rhs = jnp.concatenate(stacked(t0, 0, 256 * px) + stacked(t1, 0, 256 * px), 0)
        base = 0.08 * jnp.dot(y_mat[...], rhs, preferred_element_type=F32)
        low = 0.08 * jnp.dot(
            y_mat[:, 96:], jnp.concatenate(stacked(t0, 48, 256 * px), 0), preferred_element_type=F32
        )
        high = 0.08 * jnp.dot(
            y_mat[:, 96:], jnp.concatenate(stacked(t0, 96, 256 * px), 0), preferred_element_type=F32
        )
        out[4 * px] += base + low
        out[4 * px + 1] += base
        out[4 * px + 2] += base
        out[4 * px + 3] += base + high

    @pl.when(works)
    def _():
        counted(guesses.at[:, 0:7], line_send, line_recv).wait_send()

    @pl.when(idle)
    def _():
        counted(guesses.at[:, 0:8], line_send, line_recv).wait_send()

    for i, there in ((0, above), (1, below)):

        @pl.when(there)
        def _():
            counted(lines.at[0:9], cross_send.at[i], cross_recv).wait_send()

    for copy, _, goes in near + halo:
        pl.when(goes)(copy.wait_send)

    @pl.when(works)
    def _():
        share.wait_send()
        counted(centre.at[:, 0:15], pot_send, pot_recv).wait_send()
        counted(pot.at[0:14], pot_send, pot_recv).wait_recv()

    @pl.when(idle)
    def _():
        counted(pot.at[0:16], pot_send, pot_recv).wait_recv()

    packed = result.reshape(64, 32)
    for k in range(4):
        packed[pl.ds(k, 16, stride=4), :] = pot[:, 32 * k : 32 * k + 32]


def deliver(fine, coarse, out, pot, sem):
    copies = [pltpu.make_async_copy(fine, out, sem.at[0]), pltpu.make_async_copy(coarse, pot, sem.at[1])]
    for copy in copies:
        copy.start()
    for copy in copies:
        copy.wait()


def per_device(comp, guess):
    slabs = lax.axis_size("slab")
    dma = pltpu.SemaphoreType.DMA

    def body(*refs):
        step(slabs, *refs)

    vmem = pl.BlockSpec(memory_space=pltpu.VMEM)
    anywhere = pl.BlockSpec(memory_space=pl.ANY)
    fine, lines = pl.pallas_call(
        body,
        out_shape=(pltpu.VMEM((8, 128, 128), F32), pltpu.VMEM((32, 2, 32), F32)),
        in_specs=[pl.BlockSpec(memory_space=pltpu.HBM)] * 2,
        out_specs=(vmem, vmem),
        scratch_shapes=[
            pltpu.VMEM((12, 128, 128), F32),
            pltpu.VMEM((32, 2, 32), F32),
            pltpu.VMEM((17 + 2 * REACH, 128), F32),
            pltpu.VMEM((WINDOW, 16, 128), F32),
            pltpu.VMEM((WINDOW, 16, 128), F32),
            pltpu.VMEM((WINDOW, 16, 128), F32),
            pltpu.VMEM((10, 128, 128), F32),
            pltpu.VMEM((2, 128, 128), F32),
            pltpu.VMEM((512, 128), BF16),
            pltpu.VMEM((3, 128, 512), BF16),
            pltpu.VMEM((128, 192), BF16),
            pltpu.VMEM((16, 128), F32),
            pltpu.VMEM((64, 128), F32),
            pltpu.VMEM((2, 16, 128), F32),
            pltpu.VMEM((16, 128), F32),
            dma((2,)),
            dma,
            dma,
            dma,
            dma((2,)),
            dma,
            dma((6,)),
            dma,
            dma((2,)),
            dma((2,)),
            dma,
            dma,
            dma,
            dma,
            pltpu.SemaphoreType.REGULAR((4,)),
        ],
        compiler_params=pltpu.CompilerParams(
            collective_id=0, has_side_effects=True, vmem_limit_bytes=62 * 1024 * 1024
        ),
        name="step",
    )(comp, guess)
    return pl.pallas_call(
        deliver,
        out_shape=(jax.ShapeDtypeStruct(comp.shape, F32), jax.ShapeDtypeStruct(guess.shape, F32)),
        in_specs=[vmem, vmem],
        out_specs=(pl.BlockSpec(memory_space=pltpu.HBM),) * 2,
        scratch_shapes=[dma((2,))],
        compiler_params=pltpu.CompilerParams(vmem_limit_bytes=1024 * 1024),
        name="deliver",
    )(fine, lines)


def solution(mesh):
    placed = (P(("slab", "grp"), None, None), P("slab", "grp", None))
    return jax.shard_map(
        per_device, mesh=mesh, in_specs=placed, out_specs=placed, check_vma=False
    )
```

```python
import jax
import jax.numpy as jnp
from jax import lax
from jax.experimental import pallas as pl
from jax.experimental.pallas import tpu as pltpu
from jax.sharding import PartitionSpec as P

MESH = pl.DeviceIdType.MESH
REACH = 5
WINDOW = 2 * REACH + 2
UPPER, LOWER = (0, 2, 4), (10, 12, 14)
HUB = 8
FAR_FIRST = (8, 7, 9, 6, 10, 5, 11, 4, 12, 3, 13, 2, 14, 1, 15)
F32 = jnp.float32
BF16 = jnp.bfloat16


def iota(shape, dim):
    return lax.broadcasted_iota(jnp.int32, shape, dim)


def lanes(x, shift):
    return pltpu.roll(x, (-shift) % 128, 1)


def rows(x, shift):
    return pltpu.roll(x, (-shift) % x.shape[0], 0)


def split3(x):
    high = x.astype(BF16)
    rest = x - high.astype(F32)
    mid = rest.astype(BF16)
    low = (rest - mid.astype(F32)).astype(BF16)
    return high, mid, low


def coarse_cycle(source, guess, first_pair, pairs):
    lane, row = iota((16, 128), 1), iota((16, 128), 0)
    front, odd_row = lane < 64, lane % 64 >= 32
    zero = jnp.zeros((16, 128), F32)
    known = [(first_pair + k >= 0) & (first_pair + k < pairs) for k in range(WINDOW)]
    inside = [jnp.where(k, 1.0, 0.0).astype(F32) for k in known]
    guess = {k: jnp.where(known[k], guess[k], 0.0) for k in guess}
    source = {k: jnp.where(known[k], source[k], 0.0) for k in source}

    def above(v):
        return jnp.where(row < 15, rows(v, 1), 0.0)

    def under(v):
        return jnp.where(row > 0, rows(v, -1), 0.0)

    def neighbours(v, wanted):
        swapped = {k: pltpu.roll(v[k], 64, 1) for k in v}
        done = {}
        for k in wanted:
            line = v[k] + jnp.where(odd_row, under(v[k]), above(v[k]))
            line = jnp.where(odd_row, lanes(line, -32), lanes(line, 32))
            line += jnp.where(lane % 32 < 31, lanes(v[k], 1), 0.0)
            line += jnp.where(lane % 32 > 0, lanes(v[k], -1), 0.0)
            beside = jnp.where(front, swapped.get(k - 1, zero), swapped.get(k + 1, zero))
            done[k] = line + swapped[k] + beside
        return done

    def sweep(v, wanted):
        around = neighbours(v, wanted)
        return {k: inside[k] * (0.2 * v[k] + (0.8 / 6.5) * (source[k] + around[k])) for k in wanted}

    pre = sweep(guess, range(WINDOW))
    places = range(1, WINDOW - 1)
    around = neighbours(pre, places)
    resid = jnp.concatenate(
        [(0.05 * inside[k]) * (source[k] + around[k] - 6.5 * pre[k]) for k in places], 0
    )
    at, to = iota((256, 128), 0), iota((256, 128), 1)
    cell = jnp.where((at % 32) // 2 == (to % 32) // 2, 1.0, 0.0).astype(BF16)
    high, mid, low = split3(resid)
    cells = jnp.dot(jnp.concatenate([high, mid], 1), cell, preferred_element_type=F32)
    cells += jnp.dot(low, cell[:128], preferred_element_type=F32)
    start = {k: cells[16 * (k - 1) : 16 * k] for k in places}
    c = start
    for sweeps in range(1, 3):
        new = {}
        for k in places[sweeps : len(places) - sweeps]:
            v = c[k]
            total = c[k - 1] + c[k + 1] + above(v) + under(v)
            total += jnp.where(lane % 32 < 30, lanes(v, 2), 0.0) + jnp.where(lane % 32 > 1, lanes(v, -2), 0.0)
            new[k] = inside[k] * (0.2 * v + start[k] + 0.1 * total)
        c = new
    v = {k: pre[k] + c[k] for k in c}
    wanted = range(4, WINDOW - 4)
    v = sweep(sweep(v, wanted), wanted)
    return jnp.concatenate([v[k] for k in wanted], 0)


def three(potential, which):
    lane = iota((16, 128), 1)
    pair = [potential[16 * k : 16 * k + 16] for k in range(4)]
    own = jnp.where(which == 0, pair[1], pair[2])
    last, first = jnp.where(which == 0, pair[0], pair[1]), jnp.where(which == 0, pair[2], pair[3])
    return jnp.concatenate([own, jnp.where(lane < 64, first, last)], 0)


def plane_neighbours(v):
    row, lane = iota(v.shape, 0), iota(v.shape, 1)
    total = jnp.where(row < 127, rows(v, 1), 0.0) + jnp.where(row > 0, rows(v, -1), 0.0)
    total += jnp.where(lane < 127, lanes(v, 1), 0.0) + jnp.where(lane > 0, lanes(v, -1), 0.0)
    return total


def spread(fine, coarse):
    block, place = fine // 4, fine % 4
    same = jnp.where(block == coarse, 1.0, 0.0)
    first, last = jnp.where(place == 0, 1.0, 0.0), jnp.where(place == 3, 1.0, 0.0)
    second = -same * (first + last)
    second += first * jnp.where(block - 1 == coarse, 1.0, 0.0)
    second += last * jnp.where(block + 1 == coarse, 1.0, 0.0)
    return same, second


def step(
    slabs, comp, guess, out, result, cells, given, lines, sources, guesses, beyond, chem, sums, gather, z_mat,
    y_mat, mine, near_potential, centre, pot, cell_sem, given_sem, line_send, line_recv, cross_send, cross_recv,
    near_send, near_recv, halo_send, halo_recv, pot_send, pot_recv, share_send, share_recv, word,
):
    s, g = lax.axis_index("slab"), lax.axis_index("grp")
    me = s * 16 + g
    pairs = slabs * 16
    below, above = s > 0, s < slabs - 1
    first = g - g % 2
    second = (s == 0) & (first == 0)
    works = jnp.where(second, g == 1, g == first)
    idle = jnp.logical_not(works)
    base = s * 16 + first
    middle = slabs // 2
    late, early, hub = s == middle - 1, s == middle, (s == middle - 2) & (g == HUB)
    announce = word.at[0]
    beside = word.at[1]
    down = word.at[2]
    go = word.at[3]

    def device(d):
        return (d // 16, d % 16)

    def worker(pair):
        return device(jnp.where(pair == 0, 1, pair))

    def tell(semaphore, to):
        pl.semaphore_signal(semaphore, 1, device_id=to, device_id_type=MESH)

    halves = [
        pltpu.make_async_copy(comp.at[4 * h : 4 * h + 4], cells.at[2 + 4 * h : 6 + 4 * h], cell_sem.at[h])
        for h in range(2)
    ]
    load_guess = pltpu.make_async_copy(guess, given, given_sem)
    load_guess.start()
    for half in halves:
        half.start()

    barrier = pltpu.get_barrier_semaphore()

    @pl.when(works & jnp.logical_not(late))
    def _():
        for k in FAR_FIRST:
            tell(barrier, (s, (g + k) % 16))

    @pl.when(works & below & (g < REACH))
    def _():
        for k in FAR_FIRST + (0,):
            tell(barrier, (s - 1, (g + k) % 16))

    @pl.when(works & above & (g >= 16 - WINDOW // 2) & (s != middle - 1) & (s != middle - 2))
    def _():
        for k in FAR_FIRST + (0,):
            tell(barrier, (s + 1, (g + k) % 16))

    @pl.when(late)
    def _():
        tell(barrier, (s - 1, HUB))

    @pl.when(early & (idle | (g >= REACH)))
    def _():
        for to in LOWER:
            tell(barrier, (s - 1, to))

    @pl.when(late)
    def _():
        receives = (g == LOWER[0]) | (g == LOWER[1]) | (g == LOWER[2])
        pl.semaphore_wait(barrier, jnp.where(receives, 16, 3))

        @pl.when(receives)
        def _():
            for k in FAR_FIRST + (0,):
                tell(down, (s + 1, (g + k) % 16))

        @pl.when(g == 15)
        def _():
            tell(down, (s + 1, 0))

    lines[0:REACH] = jnp.zeros((REACH, 128), F32)
    lines[REACH + 16 :] = jnp.zeros((REACH + 1, 128), F32)
    at, lane = iota((512, 128), 0), iota((512, 128), 1)
    hit = (at // 128 == lane // 32) & (at % 128 // 4 == lane % 32)
    gather[...] = jnp.where(hit, 1.0 / 64, 0.0).astype(BF16)
    load_guess.wait()
    packed = given.reshape(64, 32)
    lines[REACH : REACH + 16] = jnp.concatenate(
        [packed[pl.ds(k, 16, stride=4), :] for k in range(4)], axis=1
    )

    def guess_up():
        for to in UPPER:
            pltpu.make_async_remote_copy(
                lines.at[16 + to : 21], beyond.at[0 : REACH - to, g], cross_send.at[0], cross_recv,
                device_id=(s + 1, to), device_id_type=MESH,
            ).start()

    def guess_down():
        for to in LOWER:
            pltpu.make_async_remote_copy(
                lines.at[REACH : to - 4], beyond.at[21 - to : WINDOW, g], cross_send.at[1], cross_recv,
                device_id=(s - 1, to), device_id_type=MESH,
            ).start()

    @pl.when(late)
    def _():
        guess_up()

    for h in range(2):
        halves[h].wait()
        own = 2 + 4 * h
        sums[h] = (cells[own] + cells[own + 1]) + (cells[own + 2] + cells[own + 3])
    parts = []
    for h in range(2):
        for half in range(2):
            parts.append(sum(sums[h, pl.ds(4 * half + j, 16, stride=8), :] for j in range(4)))
    wide = jnp.concatenate(split3(jnp.concatenate(parts, axis=1)), axis=0)
    means = jnp.dot(wide, gather[...], preferred_element_type=F32)
    means = means[:16] + means[16:32] + means[32:]
    mine[...] = means

    @pl.when(works)
    def _():
        sources[REACH + g - first] = means

    @pl.when(jnp.logical_not(late))
    def _():
        asked = 3 * (above.astype(jnp.int32) + (below & jnp.logical_not(early)).astype(jnp.int32))
        pl.semaphore_wait(barrier, 7 + idle.astype(jnp.int32) + asked + 16 * hub.astype(jnp.int32))

    @pl.when(hub)
    def _():
        for to in range(16):
            tell(go, (s + 1, to))

    near = []
    for i in (0, 5, 1, 4, 2, 3):
        o = 2 * i - 6 + g % 2
        copy = pltpu.make_async_remote_copy(
            mine, sources.at[REACH - o], near_send.at[i], near_recv,
            device_id=worker(me + o), device_id_type=MESH,
        )
        itself = works & (me + o == base)
        goes = (me + o >= 0) & (me + o < pairs) & jnp.logical_not(itself)
        near.append((copy, o, goes))
    halo = []
    for i, (o, src, dst) in enumerate(((1, comp.at[6:8], cells.at[0:2]), (-1, comp.at[0:2], cells.at[10:12]))):
        copy = pltpu.make_async_remote_copy(
            src, dst, halo_send.at[i], halo_recv.at[i], device_id=device(me + o), device_id_type=MESH
        )
        halo.append((copy, o, (me + o >= 0) & (me + o < pairs)))

    @pl.when(late)
    def _():
        for copy, o, goes in near:
            pl.when(g + o > 15)(copy.start)
        pl.when(g == 15)(halo[0][0].start)
        pl.semaphore_wait(go, 1)

    pl.when(above & jnp.logical_not(late))(guess_up)
    pl.when(below & jnp.logical_not(early))(guess_down)
    for j in (4, 3, 5, 2, 6, 1, 7, 0):
        to = (first + 2 * j) % 16
        copy = pltpu.make_async_remote_copy(
            lines.at[pl.ds(to, WINDOW)], guesses.at[:, g], line_send, line_recv,
            device_id=worker(s * 16 + to), device_id_type=MESH,
        )
        if j:
            copy.start()
        else:
            pl.when(idle)(copy.start)
    for copy, o, goes in near:
        up, under = g + o > 15, g + o < 0
        pl.when(goes & jnp.logical_not((up & late) | (under & early)))(copy.start)

    @pl.when(works)
    def _():
        guesses[:, pl.ds(g, 1), :] = lines[pl.ds(first, WINDOW), :].reshape(WINDOW, 1, 128)
        alone = (early & (g == 0)) | ((s == 0) & ((g == 1) | (g == 2)))
        pl.semaphore_wait(beside, jnp.where(alone, 1, 2))

    @pl.when(idle)
    def _():
        @pl.when(g > 0)
        def _():
            tell(beside, (s, g - 1))

        @pl.when((me < pairs - 1) & jnp.logical_not(late & (g == 15)))
        def _():
            tell(beside, device(me + 1))

        for j in (4, 3, 5, 2, 6, 1, 7, 0):
            tell(announce, worker(s * 16 + (first + 2 * j) % 16))

    for copy, o, goes in halo:
        apart = late & (g == 15) if o > 0 else early & (g == 0)
        pl.when(goes & jnp.logical_not(apart))(copy.start)

    @pl.when(early)
    def _():
        pl.semaphore_wait(down, 3 + (g == 0).astype(jnp.int32))
        guess_down()
        for copy, o, goes in near:
            pl.when(g + o < 0)(copy.start)
        pl.when(g == 0)(halo[1][0].start)

    at, lane = iota((128, 512), 0), iota((128, 512), 1)
    hit = (lane // 128 == at // 32) & (lane % 128 // 4 == at % 32)
    z_mat[0] = jnp.where(hit, 1.0, 0.0).astype(BF16)
    z_mat[1] = jnp.where(hit & (lane % 4 == 0), 1.0, 0.0).astype(BF16)
    z_mat[2] = jnp.where(hit & (lane % 4 == 3), 1.0, 0.0).astype(BF16)
    at, lane = iota((128, 192), 0), iota((128, 192), 1)
    coarse = 2 * (lane % 16) + (lane // 16) % 2
    same, second = spread(at, coarse)
    y_mat[...] = jnp.where(lane < 96, second, same).astype(BF16)

    def chemical(p):
        u = cells[p + 2]
        around = cells[p + 1] + cells[p + 3] + plane_neighbours(u)
        chem[p + 1] = u * u * u + 2.0 * u - 0.5 * around

    def partial(f):
        mu = chem[f + 1]
        around = chem[f] + chem[f + 2] + plane_neighbours(mu)
        out[f] = cells[f + 2] + 0.02 * (around - 6.0 * mu)

    lax.fori_loop(1, 7, lambda p, _: (chemical(p), 0)[1], 0)
    lax.fori_loop(2, 6, lambda f, _: (partial(f), 0)[1], 0)

    def counted(ref, send, recv):
        return pltpu.make_async_remote_copy(
            ref, ref, send, recv, device_id=(s, (g + 1) % 16), device_id_type=MESH
        )

    share = pltpu.make_async_remote_copy(
        near_potential.at[32:64], near_potential.at[0:32], share_send, share_recv,
        device_id=(s, 2 * first + 1 - g), device_id_type=MESH,
    )

    @pl.when(works)
    def _():
        counted(guesses.at[:, 0:15], line_send, line_recv).wait_recv()
        for there, spots in (
            (below, [(j, slice(0, REACH - j)) for j in UPPER]),
            (above, [(j, slice(21 - j, WINDOW)) for j in LOWER]),
        ):
            for j, spot in spots:

                @pl.when(there & (g == j))
                def _():
                    counted(beyond.at[spot], cross_send.at[0], cross_recv).wait_recv()

        lost = jnp.maximum(REACH - base, 0) + jnp.maximum(base + 7 - pairs, 0)
        for less in (0, 1, 3, 5):

            @pl.when(lost == less)
            def _():
                counted(sources.at[0 : WINDOW - 1 - less], near_send.at[0], near_recv).wait_recv()

        start = {
            k: jnp.where((first - REACH + k >= 0) & (first - REACH + k < 16), guesses[k], beyond[k]) for k in range(WINDOW)
        }
        potential = coarse_cycle({k: sources[k] for k in range(WINDOW)}, start, base - REACH, pairs)
        near_potential[0:32] = three(potential, g - first)
        near_potential[32:64] = three(potential, 1 + first - g)
        centre[...] = potential[16:48].reshape(2, 16, 128)
        pl.semaphore_wait(announce, 8)
        share.start()
        for k in FAR_FIRST:
            to = (g + k) % 16
            pltpu.make_async_remote_copy(
                centre.at[:, to], pot.at[pl.ds(first, 2)], pot_send, pot_recv,
                device_id=(s, to), device_id_type=MESH,
            ).start()
        pot[pl.ds(first, 2), :] = centre[:, pl.ds(g, 1), :].reshape(2, 128)

    for copy, o, _ in halo:
        pl.when((me - o >= 0) & (me - o < pairs))(copy.wait_recv)
    zero = jnp.zeros((2, 128, 128), F32)

    @pl.when(me == 0)
    def _():
        cells[0:2] = zero

    @pl.when(me == pairs - 1)
    def _():
        cells[10:12] = zero

    for p in (-1, 0, 7, 8):
        chemical(p)

    @pl.when(me == 0)
    def _():
        chem[0] = zero[0]

    @pl.when(me == pairs - 1)
    def _():
        chem[9] = zero[0]

    for f in (0, 1, 6, 7):
        partial(f)

    pl.when(idle)(share.wait_recv)
    own, edges = near_potential[0:16], near_potential[16:32]
    lane = iota((16, 128), 1)
    swapped, edges = pltpu.roll(own, 64, 1), pltpu.roll(edges, 64, 1)
    before = jnp.where(lane < 64, edges, swapped) - own
    after = jnp.where(lane < 64, swapped, edges) - own
    left = jnp.where(lane % 32 > 0, lanes(own, -1), 0.0) - own
    right = jnp.where(lane % 32 < 31, lanes(own, 1), 0.0) - own
    t0 = jnp.dot(
        jnp.concatenate(split3(own) + split3(before) + split3(after), 0), z_mat[0],
        preferred_element_type=F32,
    ).astype(BF16)
    t1 = jnp.dot(
        jnp.concatenate([jnp.concatenate(split3(left), 0), jnp.concatenate(split3(right), 0)], 1),
        z_mat[1:].reshape(256, 512), preferred_element_type=F32,
    ).astype(BF16)

    def stacked(t, at, column):
        return [
            t[at + 16 * i : at + 16 * i + 16, column + 128 * py : column + 128 * py + 128]
            for i in range(3)
            for py in range(2)
        ]

    for px in range(2):
        rhs = jnp.concatenate(stacked(t0, 0, 256 * px) + stacked(t1, 0, 256 * px), 0)
        base = 0.08 * jnp.dot(y_mat[...], rhs, preferred_element_type=F32)
        low = 0.08 * jnp.dot(
            y_mat[:, 96:], jnp.concatenate(stacked(t0, 48, 256 * px), 0), preferred_element_type=F32
        )
        high = 0.08 * jnp.dot(
            y_mat[:, 96:], jnp.concatenate(stacked(t0, 96, 256 * px), 0), preferred_element_type=F32
        )
        out[4 * px] += base + low
        out[4 * px + 1] += base
        out[4 * px + 2] += base
        out[4 * px + 3] += base + high

    @pl.when(works)
    def _():
        counted(guesses.at[:, 0:7], line_send, line_recv).wait_send()

    @pl.when(idle)
    def _():
        counted(guesses.at[:, 0:8], line_send, line_recv).wait_send()

    for i, there in ((0, above), (1, below)):

        @pl.when(there)
        def _():
            counted(lines.at[0:9], cross_send.at[i], cross_recv).wait_send()

    for copy, _, goes in near + halo:
        pl.when(goes)(copy.wait_send)

    @pl.when(works)
    def _():
        share.wait_send()
        counted(centre.at[:, 0:15], pot_send, pot_recv).wait_send()
        counted(pot.at[0:14], pot_send, pot_recv).wait_recv()

    @pl.when(idle)
    def _():
        counted(pot.at[0:16], pot_send, pot_recv).wait_recv()

    packed = result.reshape(64, 32)
    for k in range(4):
        packed[pl.ds(k, 16, stride=4), :] = pot[:, 32 * k : 32 * k + 32]


def deliver(fine, coarse, out, pot, sem):
    copies = [pltpu.make_async_copy(fine, out, sem.at[0]), pltpu.make_async_copy(coarse, pot, sem.at[1])]
    for copy in copies:
        copy.start()
    for copy in copies:
        copy.wait()


def per_device(comp, guess):
    slabs = lax.axis_size("slab")
    dma = pltpu.SemaphoreType.DMA

    def body(*refs):
        step(slabs, *refs)

    vmem = pl.BlockSpec(memory_space=pltpu.VMEM)
    anywhere = pl.BlockSpec(memory_space=pl.ANY)
    fine, lines = pl.pallas_call(
        body,
        out_shape=(pltpu.VMEM((8, 128, 128), F32), pltpu.VMEM((32, 2, 32), F32)),
        in_specs=[pl.BlockSpec(memory_space=pltpu.HBM)] * 2,
        out_specs=(vmem, vmem),
        scratch_shapes=[
            pltpu.VMEM((12, 128, 128), F32),
            pltpu.VMEM((32, 2, 32), F32),
            pltpu.VMEM((17 + 2 * REACH, 128), F32),
            pltpu.VMEM((WINDOW, 16, 128), F32),
            pltpu.VMEM((WINDOW, 16, 128), F32),
            pltpu.VMEM((WINDOW, 16, 128), F32),
            pltpu.VMEM((10, 128, 128), F32),
            pltpu.VMEM((2, 128, 128), F32),
            pltpu.VMEM((512, 128), BF16),
            pltpu.VMEM((3, 128, 512), BF16),
            pltpu.VMEM((128, 192), BF16),
            pltpu.VMEM((16, 128), F32),
            pltpu.VMEM((64, 128), F32),
            pltpu.VMEM((2, 16, 128), F32),
            pltpu.VMEM((16, 128), F32),
            dma((2,)),
            dma,
            dma,
            dma,
            dma((2,)),
            dma,
            dma((6,)),
            dma,
            dma((2,)),
            dma((2,)),
            dma,
            dma,
            dma,
            dma,
            pltpu.SemaphoreType.REGULAR((4,)),
        ],
        compiler_params=pltpu.CompilerParams(
            collective_id=0, has_side_effects=True, vmem_limit_bytes=62 * 1024 * 1024
        ),
        name="step",
    )(comp, guess)
    return pl.pallas_call(
        deliver,
        out_shape=(jax.ShapeDtypeStruct(comp.shape, F32), jax.ShapeDtypeStruct(guess.shape, F32)),
        in_specs=[vmem, vmem],
        out_specs=(pl.BlockSpec(memory_space=pltpu.HBM),) * 2,
        scratch_shapes=[dma((2,))],
        compiler_params=pltpu.CompilerParams(vmem_limit_bytes=1024 * 1024),
        name="deliver",
    )(fine, lines)


def solution(mesh):
    placed = (P(("slab", "grp"), None, None), P("slab", "grp", None))
    return jax.shard_map(
        per_device, mesh=mesh, in_specs=placed, out_specs=placed, check_vma=False
    )
```

```python
import jax
import jax.numpy as jnp
from jax import lax
from jax.experimental import pallas as pl
from jax.experimental.pallas import tpu as pltpu
from jax.sharding import PartitionSpec as P

MESH = pl.DeviceIdType.MESH
REACH = 5
WINDOW = 2 * REACH + 2
UPPER, LOWER = (0, 2, 4), (10, 12, 14)
HUB = 8
FAR_FIRST = (8, 7, 9, 6, 10, 5, 11, 4, 12, 3, 13, 2, 14, 1, 15)
F32 = jnp.float32
BF16 = jnp.bfloat16


def iota(shape, dim):
    return lax.broadcasted_iota(jnp.int32, shape, dim)


def lanes(x, shift):
    return pltpu.roll(x, (-shift) % 128, 1)


def rows(x, shift):
    return pltpu.roll(x, (-shift) % x.shape[0], 0)


def split3(x):
    high = x.astype(BF16)
    rest = x - high.astype(F32)
    mid = rest.astype(BF16)
    low = (rest - mid.astype(F32)).astype(BF16)
    return high, mid, low


def coarse_cycle(source, guess, first_pair, pairs):
    lane, row = iota((16, 128), 1), iota((16, 128), 0)
    front, odd_row = lane < 64, lane % 64 >= 32
    zero = jnp.zeros((16, 128), F32)
    known = [(first_pair + k >= 0) & (first_pair + k < pairs) for k in range(WINDOW)]
    inside = [jnp.where(k, 1.0, 0.0).astype(F32) for k in known]
    guess = {k: jnp.where(known[k], guess[k], 0.0) for k in guess}
    source = {k: jnp.where(known[k], source[k], 0.0) for k in source}

    def above(v):
        return jnp.where(row < 15, rows(v, 1), 0.0)

    def under(v):
        return jnp.where(row > 0, rows(v, -1), 0.0)

    def neighbours(v, wanted):
        swapped = {k: pltpu.roll(v[k], 64, 1) for k in v}
        done = {}
        for k in wanted:
            line = v[k] + jnp.where(odd_row, under(v[k]), above(v[k]))
            line = jnp.where(odd_row, lanes(line, -32), lanes(line, 32))
            line += jnp.where(lane % 32 < 31, lanes(v[k], 1), 0.0)
            line += jnp.where(lane % 32 > 0, lanes(v[k], -1), 0.0)
            beside = jnp.where(front, swapped.get(k - 1, zero), swapped.get(k + 1, zero))
            done[k] = line + swapped[k] + beside
        return done

    def sweep(v, wanted):
        around = neighbours(v, wanted)
        return {k: inside[k] * (0.2 * v[k] + (0.8 / 6.5) * (source[k] + around[k])) for k in wanted}

    pre = sweep(guess, range(WINDOW))
    places = range(1, WINDOW - 1)
    around = neighbours(pre, places)
    resid = jnp.concatenate(
        [(0.05 * inside[k]) * (source[k] + around[k] - 6.5 * pre[k]) for k in places], 0
    )
    at, to = iota((256, 128), 0), iota((256, 128), 1)
    cell = jnp.where((at % 32) // 2 == (to % 32) // 2, 1.0, 0.0).astype(BF16)
    high, mid, low = split3(resid)
    cells = jnp.dot(jnp.concatenate([high, mid], 1), cell, preferred_element_type=F32)
    cells += jnp.dot(low, cell[:128], preferred_element_type=F32)
    start = {k: cells[16 * (k - 1) : 16 * k] for k in places}
    c = start
    for sweeps in range(1, 3):
        new = {}
        for k in places[sweeps : len(places) - sweeps]:
            v = c[k]
            total = c[k - 1] + c[k + 1] + above(v) + under(v)
            total += jnp.where(lane % 32 < 30, lanes(v, 2), 0.0) + jnp.where(lane % 32 > 1, lanes(v, -2), 0.0)
            new[k] = inside[k] * (0.2 * v + start[k] + 0.1 * total)
        c = new
    v = {k: pre[k] + c[k] for k in c}
    wanted = range(4, WINDOW - 4)
    v = sweep(sweep(v, wanted), wanted)
    return jnp.concatenate([v[k] for k in wanted], 0)


def plane_neighbours(v):
    row, lane = iota(v.shape, 0), iota(v.shape, 1)
    total = jnp.where(row < 127, rows(v, 1), 0.0) + jnp.where(row > 0, rows(v, -1), 0.0)
    total += jnp.where(lane < 127, lanes(v, 1), 0.0) + jnp.where(lane > 0, lanes(v, -1), 0.0)
    return total


def spread(fine, coarse):
    block, place = fine // 4, fine % 4
    same = jnp.where(block == coarse, 1.0, 0.0)
    first, last = jnp.where(place == 0, 1.0, 0.0), jnp.where(place == 3, 1.0, 0.0)
    second = -same * (first + last)
    second += first * jnp.where(block - 1 == coarse, 1.0, 0.0)
    second += last * jnp.where(block + 1 == coarse, 1.0, 0.0)
    return same, second


def step(
    slabs, comp, guess, out, result, cells, given, lines, sources, guesses, beyond, chem, sums, gather, z_mat,
    y_mat, mine, near_potential, centre, pot, cell_sem, given_sem, line_send, line_recv, cross_send, cross_recv,
    near_send, near_recv, halo_send, halo_recv, pot_send, pot_recv, share_send, share_recv, word,
):
    s, g = lax.axis_index("slab"), lax.axis_index("grp")
    me = s * 16 + g
    pairs = slabs * 16
    below, above = s > 0, s < slabs - 1
    first = g - g % 2
    second = (s == 0) & (first == 0)
    works = jnp.where(second, g == 1, g == first)
    idle = jnp.logical_not(works)
    base = s * 16 + first
    middle = slabs // 2
    late, early, hub = s == middle - 1, s == middle, (s == middle - 2) & (g == HUB)
    announce = word.at[0]
    beside = word.at[1]
    down = word.at[2]
    go = word.at[3]

    def device(d):
        return (d // 16, d % 16)

    def worker(pair):
        return device(jnp.where(pair == 0, 1, pair))

    def tell(semaphore, to):
        pl.semaphore_signal(semaphore, 1, device_id=to, device_id_type=MESH)

    halves = [
        pltpu.make_async_copy(comp.at[4 * h : 4 * h + 4], cells.at[2 + 4 * h : 6 + 4 * h], cell_sem.at[h])
        for h in range(2)
    ]
    load_guess = pltpu.make_async_copy(guess, given, given_sem)
    load_guess.start()
    for half in halves:
        half.start()

    barrier = pltpu.get_barrier_semaphore()

    @pl.when(works & jnp.logical_not(late))
    def _():
        for k in FAR_FIRST:
            tell(barrier, (s, (g + k) % 16))

    @pl.when(works & below & (g < REACH))
    def _():
        for k in FAR_FIRST + (0,):
            tell(barrier, (s - 1, (g + k) % 16))

    @pl.when(works & above & (g >= 16 - WINDOW // 2) & (s != middle - 1) & (s != middle - 2))
    def _():
        for k in FAR_FIRST + (0,):
            tell(barrier, (s + 1, (g + k) % 16))

    @pl.when(late)
    def _():
        tell(barrier, (s - 1, HUB))

    @pl.when(early & (idle | (g >= REACH)))
    def _():
        for to in LOWER:
            tell(barrier, (s - 1, to))

    @pl.when(late)
    def _():
        receives = (g == LOWER[0]) | (g == LOWER[1]) | (g == LOWER[2])
        pl.semaphore_wait(barrier, jnp.where(receives, 16, 3))

        @pl.when(receives)
        def _():
            for k in FAR_FIRST + (0,):
                tell(down, (s + 1, (g + k) % 16))

        @pl.when(g == 15)
        def _():
            tell(down, (s + 1, 0))

    lines[0:REACH] = jnp.zeros((REACH, 128), F32)
    lines[REACH + 16 :] = jnp.zeros((REACH + 1, 128), F32)
    at, lane = iota((512, 128), 0), iota((512, 128), 1)
    hit = (at // 128 == lane // 32) & (at % 128 // 4 == lane % 32)
    gather[...] = jnp.where(hit, 1.0 / 64, 0.0).astype(BF16)
    load_guess.wait()
    packed = given.reshape(64, 32)
    lines[REACH : REACH + 16] = jnp.concatenate(
        [packed[pl.ds(k, 16, stride=4), :] for k in range(4)], axis=1
    )

    def guess_up():
        for to in UPPER:
            pltpu.make_async_remote_copy(
                lines.at[16 + to : 21], beyond.at[0 : REACH - to, g], cross_send.at[0], cross_recv,
                device_id=(s + 1, to), device_id_type=MESH,
            ).start()

    def guess_down():
        for to in LOWER:
            pltpu.make_async_remote_copy(
                lines.at[REACH : to - 4], beyond.at[21 - to : WINDOW, g], cross_send.at[1], cross_recv,
                device_id=(s - 1, to), device_id_type=MESH,
            ).start()

    @pl.when(late)
    def _():
        guess_up()

    for h in range(2):
        halves[h].wait()
        own = 2 + 4 * h
        sums[h] = (cells[own] + cells[own + 1]) + (cells[own + 2] + cells[own + 3])
    parts = []
    for h in range(2):
        for half in range(2):
            parts.append(sum(sums[h, pl.ds(4 * half + j, 16, stride=8), :] for j in range(4)))
    wide = jnp.concatenate(split3(jnp.concatenate(parts, axis=1)), axis=0)
    means = jnp.dot(wide, gather[...], preferred_element_type=F32)
    means = means[:16] + means[16:32] + means[32:]
    mine[...] = means

    @pl.when(works)
    def _():
        sources[REACH + g - first] = means

    @pl.when(jnp.logical_not(late))
    def _():
        asked = 3 * (above.astype(jnp.int32) + (below & jnp.logical_not(early)).astype(jnp.int32))
        pl.semaphore_wait(barrier, 7 + idle.astype(jnp.int32) + asked + 16 * hub.astype(jnp.int32))

    @pl.when(hub)
    def _():
        for to in range(16):
            tell(go, (s + 1, to))

    near = []
    for i in (0, 5, 1, 4, 2, 3):
        o = 2 * i - 6 + g % 2
        copy = pltpu.make_async_remote_copy(
            mine, sources.at[REACH - o], near_send.at[i], near_recv,
            device_id=worker(me + o), device_id_type=MESH,
        )
        itself = works & (me + o == base)
        goes = (me + o >= 0) & (me + o < pairs) & jnp.logical_not(itself)
        near.append((copy, o, goes))
    halo = []
    for i, (o, src, dst) in enumerate(((1, comp.at[6:8], cells.at[0:2]), (-1, comp.at[0:2], cells.at[10:12]))):
        copy = pltpu.make_async_remote_copy(
            src, dst, halo_send.at[i], halo_recv.at[i], device_id=device(me + o), device_id_type=MESH
        )
        halo.append((copy, o, (me + o >= 0) & (me + o < pairs)))

    @pl.when(late)
    def _():
        for copy, o, goes in near:
            pl.when(g + o > 15)(copy.start)
        pl.when(g == 15)(halo[0][0].start)
        pl.semaphore_wait(go, 1)

    pl.when(above & jnp.logical_not(late))(guess_up)
    pl.when(below & jnp.logical_not(early))(guess_down)
    for j in (4, 3, 5, 2, 6, 1, 7, 0):
        to = (first + 2 * j) % 16
        copy = pltpu.make_async_remote_copy(
            lines.at[pl.ds(to, WINDOW)], guesses.at[:, g], line_send, line_recv,
            device_id=worker(s * 16 + to), device_id_type=MESH,
        )
        if j:
            copy.start()
        else:
            pl.when(idle)(copy.start)
    for copy, o, goes in near:
        up, under = g + o > 15, g + o < 0
        pl.when(goes & jnp.logical_not((up & late) | (under & early)))(copy.start)

    @pl.when(works)
    def _():
        guesses[:, pl.ds(g, 1), :] = lines[pl.ds(first, WINDOW), :].reshape(WINDOW, 1, 128)
        alone = (early & (g == 0)) | ((s == 0) & ((g == 1) | (g == 2)))
        pl.semaphore_wait(beside, jnp.where(alone, 1, 2))

    @pl.when(idle)
    def _():
        @pl.when(g > 0)
        def _():
            tell(beside, (s, g - 1))

        @pl.when((me < pairs - 1) & jnp.logical_not(late & (g == 15)))
        def _():
            tell(beside, device(me + 1))

        for j in (4, 3, 5, 2, 6, 1, 7, 0):
            tell(announce, worker(s * 16 + (first + 2 * j) % 16))

    for copy, o, goes in halo:
        apart = late & (g == 15) if o > 0 else early & (g == 0)
        pl.when(goes & jnp.logical_not(apart))(copy.start)

    @pl.when(early)
    def _():
        pl.semaphore_wait(down, 3 + (g == 0).astype(jnp.int32))
        guess_down()
        for copy, o, goes in near:
            pl.when(g + o < 0)(copy.start)
        pl.when(g == 0)(halo[1][0].start)

    at, lane = iota((128, 512), 0), iota((128, 512), 1)
    hit = (lane // 128 == at // 32) & (lane % 128 // 4 == at % 32)
    z_mat[0] = jnp.where(hit, 1.0, 0.0).astype(BF16)
    z_mat[1] = jnp.where(hit & (lane % 4 == 0), 1.0, 0.0).astype(BF16)
    z_mat[2] = jnp.where(hit & (lane % 4 == 3), 1.0, 0.0).astype(BF16)
    at, lane = iota((128, 192), 0), iota((128, 192), 1)
    coarse = 2 * (lane % 16) + (lane // 16) % 2
    same, second = spread(at, coarse)
    y_mat[...] = jnp.where(lane < 96, second, same).astype(BF16)

    def chemical(p):
        u = cells[p + 2]
        around = cells[p + 1] + cells[p + 3] + plane_neighbours(u)
        chem[p + 1] = u * u * u + 2.0 * u - 0.5 * around

    def partial(f):
        mu = chem[f + 1]
        around = chem[f] + chem[f + 2] + plane_neighbours(mu)
        out[f] = cells[f + 2] + 0.02 * (around - 6.0 * mu)

    lax.fori_loop(1, 7, lambda p, _: (chemical(p), 0)[1], 0)
    lax.fori_loop(2, 6, lambda f, _: (partial(f), 0)[1], 0)

    def counted(ref, send, recv):
        return pltpu.make_async_remote_copy(
            ref, ref, send, recv, device_id=(s, (g + 1) % 16), device_id_type=MESH
        )

    share = pltpu.make_async_remote_copy(
        near_potential.at[pl.ds(16 * (1 + first - g), 48)], near_potential.at[0:48], share_send, share_recv,
        device_id=(s, 2 * first + 1 - g), device_id_type=MESH,
    )

    @pl.when(works)
    def _():
        counted(guesses.at[:, 0:15], line_send, line_recv).wait_recv()
        for there, spots in (
            (below, [(j, slice(0, REACH - j)) for j in UPPER]),
            (above, [(j, slice(21 - j, WINDOW)) for j in LOWER]),
        ):
            for j, spot in spots:

                @pl.when(there & (g == j))
                def _():
                    counted(beyond.at[spot], cross_send.at[0], cross_recv).wait_recv()

        lost = jnp.maximum(REACH - base, 0) + jnp.maximum(base + 7 - pairs, 0)
        for less in (0, 1, 3, 5):

            @pl.when(lost == less)
            def _():
                counted(sources.at[0 : WINDOW - 1 - less], near_send.at[0], near_recv).wait_recv()

        start = {
            k: jnp.where((first - REACH + k >= 0) & (first - REACH + k < 16), guesses[k], beyond[k]) for k in range(WINDOW)
        }
        potential = coarse_cycle({k: sources[k] for k in range(WINDOW)}, start, base - REACH, pairs)
        near_potential[...] = potential
        centre[...] = potential[16:48].reshape(2, 16, 128)
        pl.semaphore_wait(announce, 8)
        share.start()
        for k, close in zip(FAR_FIRST, reversed(FAR_FIRST)):
            to = (g + jnp.where(early, close, k)) % 16
            pltpu.make_async_remote_copy(
                centre.at[:, to], pot.at[pl.ds(first, 2)], pot_send, pot_recv,
                device_id=(s, to), device_id_type=MESH,
            ).start()
        pot[pl.ds(first, 2), :] = centre[:, pl.ds(g, 1), :].reshape(2, 128)

    for copy, o, _ in halo:
        pl.when((me - o >= 0) & (me - o < pairs))(copy.wait_recv)
    zero = jnp.zeros((2, 128, 128), F32)

    @pl.when(me == 0)
    def _():
        cells[0:2] = zero

    @pl.when(me == pairs - 1)
    def _():
        cells[10:12] = zero

    for p in (-1, 0, 7, 8):
        chemical(p)

    @pl.when(me == 0)
    def _():
        chem[0] = zero[0]

    @pl.when(me == pairs - 1)
    def _():
        chem[9] = zero[0]

    for f in (0, 1, 6, 7):
        partial(f)

    pl.when(idle)(share.wait_recv)
    potential = near_potential[pl.ds(jnp.where(works, 16 * (g - first), 0), 48), :]
    own = potential[16:32]
    lane = iota((16, 128), 1)
    swapped = pltpu.roll(potential, 64, 1)
    before = jnp.where(lane < 64, swapped[:16], swapped[16:32]) - own
    after = jnp.where(lane < 64, swapped[16:32], swapped[32:]) - own
    left = jnp.where(lane % 32 > 0, lanes(own, -1), 0.0) - own
    right = jnp.where(lane % 32 < 31, lanes(own, 1), 0.0) - own
    t0 = jnp.dot(
        jnp.concatenate(split3(own) + split3(before) + split3(after), 0), z_mat[0],
        preferred_element_type=F32,
    ).astype(BF16)
    t1 = jnp.dot(
        jnp.concatenate([jnp.concatenate(split3(left), 0), jnp.concatenate(split3(right), 0)], 1),
        z_mat[1:].reshape(256, 512), preferred_element_type=F32,
    ).astype(BF16)

    def stacked(t, at, column):
        return [
            t[at + 16 * i : at + 16 * i + 16, column + 128 * py : column + 128 * py + 128]
            for i in range(3)
            for py in range(2)
        ]

    for px in range(2):
        rhs = jnp.concatenate(stacked(t0, 0, 256 * px) + stacked(t1, 0, 256 * px), 0)
        base = 0.08 * jnp.dot(y_mat[...], rhs, preferred_element_type=F32)
        low = 0.08 * jnp.dot(
            y_mat[:, 96:], jnp.concatenate(stacked(t0, 48, 256 * px), 0), preferred_element_type=F32
        )
        high = 0.08 * jnp.dot(
            y_mat[:, 96:], jnp.concatenate(stacked(t0, 96, 256 * px), 0), preferred_element_type=F32
        )
        out[4 * px] += base + low
        out[4 * px + 1] += base
        out[4 * px + 2] += base
        out[4 * px + 3] += base + high

    @pl.when(works)
    def _():
        counted(guesses.at[:, 0:7], line_send, line_recv).wait_send()

    @pl.when(idle)
    def _():
        counted(guesses.at[:, 0:8], line_send, line_recv).wait_send()

    for i, there in ((0, above), (1, below)):

        @pl.when(there)
        def _():
            counted(lines.at[0:9], cross_send.at[i], cross_recv).wait_send()

    for copy, _, goes in near + halo:
        pl.when(goes)(copy.wait_send)

    @pl.when(works)
    def _():
        share.wait_send()
        counted(centre.at[:, 0:15], pot_send, pot_recv).wait_send()
        counted(pot.at[0:14], pot_send, pot_recv).wait_recv()

    @pl.when(idle)
    def _():
        counted(pot.at[0:16], pot_send, pot_recv).wait_recv()

    packed = result.reshape(64, 32)
    for k in range(4):
        packed[pl.ds(k, 16, stride=4), :] = pot[:, 32 * k : 32 * k + 32]


def deliver(fine, coarse, out, pot, sem):
    copies = [pltpu.make_async_copy(fine, out, sem.at[0]), pltpu.make_async_copy(coarse, pot, sem.at[1])]
    for copy in copies:
        copy.start()
    for copy in copies:
        copy.wait()


def per_device(comp, guess):
    slabs = lax.axis_size("slab")
    dma = pltpu.SemaphoreType.DMA

    def body(*refs):
        step(slabs, *refs)

    vmem = pl.BlockSpec(memory_space=pltpu.VMEM)
    anywhere = pl.BlockSpec(memory_space=pl.ANY)
    fine, lines = pl.pallas_call(
        body,
        out_shape=(pltpu.VMEM((8, 128, 128), F32), pltpu.VMEM((32, 2, 32), F32)),
        in_specs=[pl.BlockSpec(memory_space=pltpu.HBM)] * 2,
        out_specs=(vmem, vmem),
        scratch_shapes=[
            pltpu.VMEM((12, 128, 128), F32),
            pltpu.VMEM((32, 2, 32), F32),
            pltpu.VMEM((17 + 2 * REACH, 128), F32),
            pltpu.VMEM((WINDOW, 16, 128), F32),
            pltpu.VMEM((WINDOW, 16, 128), F32),
            pltpu.VMEM((WINDOW, 16, 128), F32),
            pltpu.VMEM((10, 128, 128), F32),
            pltpu.VMEM((2, 128, 128), F32),
            pltpu.VMEM((512, 128), BF16),
            pltpu.VMEM((3, 128, 512), BF16),
            pltpu.VMEM((128, 192), BF16),
            pltpu.VMEM((16, 128), F32),
            pltpu.VMEM((64, 128), F32),
            pltpu.VMEM((2, 16, 128), F32),
            pltpu.VMEM((16, 128), F32),
            dma((2,)),
            dma,
            dma,
            dma,
            dma((2,)),
            dma,
            dma((6,)),
            dma,
            dma((2,)),
            dma((2,)),
            dma,
            dma,
            dma,
            dma,
            pltpu.SemaphoreType.REGULAR((4,)),
        ],
        compiler_params=pltpu.CompilerParams(
            collective_id=0, has_side_effects=True, vmem_limit_bytes=62 * 1024 * 1024
        ),
        name="step",
    )(comp, guess)
    return pl.pallas_call(
        deliver,
        out_shape=(jax.ShapeDtypeStruct(comp.shape, F32), jax.ShapeDtypeStruct(guess.shape, F32)),
        in_specs=[vmem, vmem],
        out_specs=(pl.BlockSpec(memory_space=pltpu.HBM),) * 2,
        scratch_shapes=[dma((2,))],
        compiler_params=pltpu.CompilerParams(vmem_limit_bytes=1024 * 1024),
        name="deliver",
    )(fine, lines)


def solution(mesh):
    placed = (P(("slab", "grp"), None, None), P("slab", "grp", None))
    return jax.shard_map(
        per_device, mesh=mesh, in_specs=placed, out_specs=placed, check_vma=False
    )
```
